32 devices in a mesh: dp: 16 (over z, y, x), tensor: 2 (over core).
Axes of the slice: x: 2, y: 2, z: 4, core: 2. Of those that a mesh axis runs over, the one named last changes fastest.
Arguments:
- image_in: bfloat16 [3200, 768], P(('dp', 'tensor')), may hold values from -6 to 6
- image_norm_gain: float32 [2, 2, 768], replicated, may hold values from 0.25 to 1.75
- image_norm_shift: float32 [2, 2, 768], replicated, may hold values from -3 to 3
- image_qkv: bfloat16 [2, 3, 768, 768], P(None, None, None, 'tensor'), may hold values from -0.21875 to 0.21875
- image_qv_bias: float32 [2, 2, 768], P(None, None, 'tensor'), may hold values from -3 to 3
- image_out_proj: bfloat16 [2, 768, 768], P(None, 'tensor'), may hold values from -0.875 to 0.875
- image_fc_in: bfloat16 [2, 768, 3072], P(None, None, 'tensor'), may hold values from -0.21875 to 0.21875
- image_fc_in_bias: float32 [2, 3072], P(None, 'tensor'), may hold values from -3 to 3
- image_fc_out: bfloat16 [2, 3072, 768], P(None, 'tensor'), may hold values from -0.109375 to 0.109375
- image_res_bias: float32 [2, 2, 768], replicated, may hold values from -3 to 3
- image_cot: float32 [3200, 768], P(('dp', 'tensor')), may hold values from -6 to 6
- caption_in: bfloat16 [2464, 512], P(('dp', 'tensor')), may hold values from -6 to 6
- caption_norm_gain: float32 [2, 2, 512], replicated, may hold values from 0.25 to 1.75
- caption_norm_shift: float32 [2, 2, 512], replicated, may hold values from -3 to 3
- caption_qkv: bfloat16 [2, 3, 512, 512], P(None, None, None, 'tensor'), may hold values from -0.25 to 0.25
- caption_qv_bias: float32 [2, 2, 512], P(None, None, 'tensor'), may hold values from -3 to 3
- caption_out_proj: bfloat16 [2, 512, 512], P(None, 'tensor'), may hold values from -1 to 1
- caption_fc_in: bfloat16 [2, 512, 2048], P(None, None, 'tensor'), may hold values from -0.25 to 0.25
- caption_fc_in_bias: float32 [2, 2048], P(None, 'tensor'), may hold values from -3 to 3
- caption_fc_out: bfloat16 [2, 2048, 512], P(None, 'tensor'), may hold values from -0.125 to 0.125
- caption_res_bias: float32 [2, 2, 512], replicated, may hold values from -3 to 3
- caption_lengths: int32 [32], P('dp'), may hold values from 5 to 77, as said below
- caption_cot: float32 [2464, 512], P(('dp', 'tensor')), may hold values from -6 to 6
Outputs:
- image_out: float32 [3200, 768], P(('dp', 'tensor'))
- image_in_grad: float32 [3200, 768], P(('dp', 'tensor'))
- image_norm_gain_grad: float32 [2, 2, 768], replicated
- image_norm_shift_grad: float32 [2, 2, 768], replicated
- image_qkv_grad: float32 [2, 3, 768, 768], P(None, None, 'dp', 'tensor')
- image_qv_bias_grad: float32 [2, 2, 768], replicated
- image_out_proj_grad: float32 [2, 768, 768], P(None, 'tensor', 'dp')
- image_fc_in_grad: float32 [2, 768, 3072], P(None, 'dp', 'tensor')
- image_fc_in_bias_grad: float32 [2, 3072], replicated
- image_fc_out_grad: float32 [2, 3072, 768], P(None, 'tensor', 'dp')
- image_res_bias_grad: float32 [2, 2, 768], replicated
- caption_out: float32 [2464, 512], P(('dp', 'tensor'))
- caption_in_grad: float32 [2464, 512], P(('dp', 'tensor'))
- caption_norm_gain_grad: float32 [2, 2, 512], replicated
- caption_norm_shift_grad: float32 [2, 2, 512], replicated
- caption_qkv_grad: float32 [2, 3, 512, 512], P(None, None, 'dp', 'tensor')
- caption_qv_bias_grad: float32 [2, 2, 512], replicated
- caption_out_proj_grad: float32 [2, 512, 512], P(None, 'tensor', 'dp')
- caption_fc_in_grad: float32 [2, 512, 2048], P(None, 'dp', 'tensor')
- caption_fc_in_bias_grad: float32 [2, 2048], replicated
- caption_fc_out_grad: float32 [2, 2048, 512], P(None, 'tensor', 'dp')
- caption_res_bias_grad: float32 [2, 2, 512], replicated
The draws below stay inside these ranges and needn't reach their ends.
Inputs may be any that keep to these rules, and one draw needn't show every extreme that they name: `caption_lengths`: each caption's number of tokens; some caption has all 77.
All inputs are finite; a program needn't handle non-finite values.
Results may differ from the reference program's by a relative error of at most 0.02.
Values may be sent and summed in bfloat16 or wider, within the bound.
No kernel may reach another device: no remote copies, remote signals or barrier semaphores. Data moves between devices by JAX's collectives and lax.ppermute only.
A program may use at most 192 MiB of HBM per device.

```python
import jax
import jax.numpy as jnp
from jax import lax

DI = 768
FI = 3072
DT = 512
FT = 2048
HEAD = 64
PATCHES = 50
CTX = 77
LAYERS = 2
IMG_DEV = 4
CAP_DEV = 2
IMAGES = 64
CAPTIONS = 32


def draw_caption_lengths(key, part):
    key = jax.random.fold_in(key, 7)
    first_key, second_key = jax.random.split(key)
    drawn = jax.random.randint(first_key, (CAPTIONS,), 5, CTX + 1)
    chosen = jax.random.randint(second_key, (), 0, CAPTIONS)
    return jnp.where(jnp.arange(CAPTIONS) == chosen, CTX, drawn).astype(jnp.int32)


def with_spikes(entries, rng, source, target, shards_of, factor):
    owner, partner = [(jnp.arange(entries.shape[axis_at]) // (entries.shape[axis_at] // shards_of)).reshape([-1 if axis == axis_at else 1 for axis in range(entries.ndim)]) for axis_at in (source, target)]
    chosen = jax.random.permutation(rng, shards_of)[partner]
    strong = (owner == chosen) | (owner == (partner + shards_of // 2) % shards_of)
    return jnp.where(strong, factor * entries, entries)


def level_of(rng, dims, cuts, smallest, largest):
    factor_of = 1.0
    for position, blocks in cuts:
        steps = jax.random.uniform(jax.random.fold_in(jax.random.fold_in(rng, 6), position), (blocks,), jnp.float32, smallest / len(cuts), largest / len(cuts))
        factor_of = factor_of * jnp.repeat(jnp.exp(steps), dims[position] // blocks).reshape((-1,) + (1,) * (len(dims) - 1 - position))
    return factor_of


def scatter_about(rng, shape, scale, reach, cuts=(), held_as=jnp.bfloat16):
    entries = jax.random.normal(rng, shape, jnp.float32) * scale
    if len(cuts) > 0:
        entries = level_of(rng, shape, cuts, -0.22, 0.18) * entries
    return jnp.clip(entries, min=-reach, max=reach).astype(held_as)


def gaussian_with(own_key, dims, scale, most, cuts, heavy, kind=jnp.bfloat16):
    values = scale * jax.random.normal(own_key, dims, jnp.float32)
    if cuts:
        values = values * level_of(own_key, dims, cuts, -0.22, 0.18)
    return jnp.clip(with_spikes(values, jax.random.fold_in(own_key, 3), *heavy), -most, most).astype(kind)


def setup_inputs(seed: int = 0) -> dict:
    key_list = jax.random.split(jax.random.key(seed), 24)
    return {
        "image_in": scatter_about(key_list[0], (IMAGES * PATCHES, DI), 1.0, 6.0, ((0, 32),)),
        "image_norm_gain": jnp.clip(1.0 + 0.15 * jax.random.normal(key_list[1], (LAYERS, 2, DI), jnp.float32), 0.25, 1.75),
        "image_norm_shift": scatter_about(key_list[2], (LAYERS, 2, DI), 0.3, 3.0, (), jnp.float32),
        "image_qkv": scatter_about(key_list[3], (LAYERS, 3, DI, DI), DI ** -0.5, 0.21875, ((3, 2),)),
        "image_qv_bias": scatter_about(key_list[4], (LAYERS, 2, DI), 0.3, 3.0, ((2, 2),), jnp.float32),
        "image_out_proj": scatter_about(key_list[5], (LAYERS, DI, DI), (DI // 16) ** -0.5, 0.875, ((1, 2),)),
        "image_fc_in": scatter_about(key_list[6], (LAYERS, DI, FI), DI ** -0.5, 0.21875, ((2, 2),)),
        "image_fc_in_bias": scatter_about(key_list[7], (LAYERS, FI), 0.3, 3.0, ((1, 2),), jnp.float32),
        "image_fc_out": scatter_about(key_list[8], (LAYERS, FI, DI), FI ** -0.5, 0.109375, ((1, 2),)),
        "image_res_bias": scatter_about(key_list[9], (LAYERS, 2, DI), 0.3, 3.0, (), jnp.float32),
        "image_cot": gaussian_with(key_list[10], (IMAGES * PATCHES, DI), 1.0, 6.0, ((0, 32),), (0, 1, 32, 2.75), jnp.float32),
        "caption_in": scatter_about(key_list[11], (CAPTIONS * CTX, DT), 1.0, 6.0, ((0, 32),)),
        "caption_norm_gain": jnp.clip(1.0 + 0.15 * jax.random.normal(key_list[12], (LAYERS, 2, DT), jnp.float32), 0.25, 1.75),
        "caption_norm_shift": scatter_about(key_list[13], (LAYERS, 2, DT), 0.3, 3.0, (), jnp.float32),
        "caption_qkv": scatter_about(key_list[14], (LAYERS, 3, DT, DT), DT ** -0.5, 0.25, ((3, 2),)),
        "caption_qv_bias": scatter_about(key_list[15], (LAYERS, 2, DT), 0.3, 3.0, ((2, 2),), jnp.float32),
        "caption_out_proj": scatter_about(key_list[16], (LAYERS, DT, DT), (DT // 16) ** -0.5, 1.0, ((1, 2),)),
        "caption_fc_in": scatter_about(key_list[17], (LAYERS, DT, FT), DT ** -0.5, 0.25, ((2, 2),)),
        "caption_fc_in_bias": scatter_about(key_list[18], (LAYERS, FT), 0.3, 3.0, ((1, 2),), jnp.float32),
        "caption_fc_out": scatter_about(key_list[19], (LAYERS, FT, DT), FT ** -0.5, 0.125, ((1, 2),)),
        "caption_res_bias": scatter_about(key_list[20], (LAYERS, 2, DT), 0.3, 3.0, (), jnp.float32),
        "caption_lengths": draw_caption_lengths(jax.random.fold_in(key_list[23], 71), 0),
        "caption_cot": gaussian_with(key_list[22], (CAPTIONS * CTX, DT), 1.0, 6.0, ((0, 32),), (0, 1, 32, 2.75), jnp.float32),
    }


EPS = 1e-05
HIGH = lax.Precision.HIGHEST

@jax.custom_vjp
def low(v):
    return lax.optimization_barrier(v.astype(jnp.bfloat16)).astype(jnp.float32)

@jax.custom_vjp
def low_back(v):
    return v

def low_keep(v):
    return (low(v), None)

def low_pass(kept, grad):
    return (grad,)

def back_keep(v):
    return (v, None)

def back_low(kept, grad):
    return (low(grad),)
low.defvjp(low_keep, low_pass)
low_back.defvjp(back_keep, back_low)

def product(first, second):
    return jnp.dot(first, second, precision=HIGH, preferred_element_type=jnp.float32)

def layer_norm(values, norm_gain, norm_shift):
    centred = values - lax.optimization_barrier(jnp.mean(values, axis=-1, keepdims=True))
    spread = lax.optimization_barrier(jnp.mean(centred * centred, axis=-1, keepdims=True))
    return centred * lax.rsqrt(spread + EPS) * norm_gain + norm_shift

def attention(query_rows, key_rows, value_rows, allowed):
    groups = allowed.shape[0]
    seq_len = allowed.shape[-1]
    heads = query_rows.shape[-1] // HEAD

    def split_heads(values):
        return values.reshape(groups, seq_len, heads, HEAD)
    scores = low_back(jnp.einsum('gqhe,gkhe->ghqk', split_heads(query_rows), split_heads(key_rows), precision=HIGH) * HEAD ** (-0.5))
    scores = jnp.where(allowed, scores, -1000000000.0)
    highest = lax.optimization_barrier(jnp.max(scores, axis=-1, keepdims=True))
    weights = jnp.exp(scores - highest)
    probs = low(weights / lax.optimization_barrier(jnp.sum(weights, axis=-1, keepdims=True)))
    mixed = jnp.einsum('ghqk,gkhe->gqhe', probs, split_heads(value_rows), precision=HIGH)
    return low_back(low(mixed.reshape(groups * seq_len, heads * HEAD)))

def block(inputs, index, params, allowed):
    norm_gain, norm_shift, w_qkv, qv_bias, out_proj, fc_in, fc_in_bias, fc_out, res_bias = params
    normed = low(layer_norm(inputs, norm_gain[index, 0], norm_shift[index, 0]))
    query_rows = low_back(low(product(normed, w_qkv[index, 0]) + qv_bias[index, 0]))
    key_rows = low_back(low(product(normed, w_qkv[index, 1])))
    value_rows = low_back(low(product(normed, w_qkv[index, 2]) + qv_bias[index, 1]))
    mixed = attention(query_rows, key_rows, value_rows, allowed)
    middle = inputs + low_back(product(mixed, out_proj[index])) + res_bias[index, 0]
    normed_two = low(layer_norm(middle, norm_gain[index, 1], norm_shift[index, 1]))
    hidden = low_back(product(normed_two, fc_in[index]) + fc_in_bias[index])
    active = low(hidden * jax.nn.sigmoid(1.702 * hidden))
    return middle + low_back(product(active, fc_out[index])) + res_bias[index, 1]

def run_tower(inputs, params, cotangent, allowed, group):
    total_rows, width = inputs.shape
    seq_len = allowed.shape[-1]
    blocks = total_rows // (group * seq_len)
    weights = tuple((member.astype(jnp.float32) for member in params))

    def forward(state, weight_set, mask):
        for index in range(LAYERS):
            state = block(state, index, weight_set, mask)
        return state

    def visit(carry, item):
        block_in, block_cot, mask = item
        output, pull = jax.vjp(lambda state, weight_set: forward(state, weight_set, mask), block_in, weights)
        grad_in, grad_weights = pull(block_cot)
        return (jax.tree.map(jnp.add, carry, grad_weights), (output, grad_in))
    initial = jax.tree.map(jnp.zeros_like, weights)
    stacked_in = inputs.astype(jnp.float32).reshape(blocks, group * seq_len, width)
    stacked_cot = cotangent.astype(jnp.float32).reshape(blocks, group * seq_len, width)
    stacked_mask = allowed.reshape(blocks, group, 1, seq_len, seq_len)
    sums, (outputs, grads) = lax.scan(visit, initial, (stacked_in, stacked_cot, stacked_mask))
    return (outputs.reshape(total_rows, width), grads.reshape(total_rows, width)) + tuple(sums)

def reference(image_in, image_norm_gain, image_norm_shift, image_qkv, image_qv_bias, image_out_proj, image_fc_in, image_fc_in_bias, image_fc_out, image_res_bias, image_cot, caption_in, caption_norm_gain, caption_norm_shift, caption_qkv, caption_qv_bias, caption_out_proj, caption_fc_in, caption_fc_in_bias, caption_fc_out, caption_res_bias, caption_lengths, caption_cot):
    image_mask = jnp.ones((IMAGES, 1, PATCHES, PATCHES), dtype=jnp.bool_)
    spots = jnp.arange(CTX).astype(jnp.int32)
    caption_mask = (spots[None, None, None, :] <= spots[None, None, :, None]) & (spots[None, None, None, :] < caption_lengths.astype(jnp.int32)[:, None, None, None])
    image_part = run_tower(image_in, (image_norm_gain, image_norm_shift, image_qkv, image_qv_bias, image_out_proj, image_fc_in, image_fc_in_bias, image_fc_out, image_res_bias), image_cot, image_mask, 4 * IMG_DEV)
    caption_part = run_tower(caption_in, (caption_norm_gain, caption_norm_shift, caption_qkv, caption_qv_bias, caption_out_proj, caption_fc_in, caption_fc_in_bias, caption_fc_out, caption_res_bias), caption_cot, caption_mask, 4 * CAP_DEV)
    return (image_part[0], image_part[1], image_part[2], image_part[3], image_part[4], image_part[5], image_part[6], image_part[7], image_part[8], image_part[9], image_part[10], caption_part[0], caption_part[1], caption_part[2], caption_part[3], caption_part[4], caption_part[5], caption_part[6], caption_part[7], caption_part[8], caption_part[9], caption_part[10])
```

```python
import jax
import jax.numpy as jnp
from jax import lax
from jax.sharding import PartitionSpec as P

DI = 768
FI = 3072
DT = 512
FT = 2048
HEAD = 64
PATCHES = 50
CTX = 77


EPS = 1e-05


def layer_norm(values, norm_gain, norm_shift):
    centred = values - jnp.mean(values, axis=-1, keepdims=True)
    spread = jnp.mean(centred * centred, axis=-1, keepdims=True)
    return centred * lax.rsqrt(spread + EPS) * norm_gain + norm_shift


def dot_plain(first, second):
    return jnp.dot(first, second, preferred_element_type=jnp.float32)


def dot_back(first, second):
    return lax.dot_general(
        first, second, (((1,), (1,)), ((), ())), preferred_element_type=jnp.float32
    )


def dot_over(first, second):
    return lax.dot_general(
        first, second, (((0,), (0,)), ((), ())), preferred_element_type=jnp.float32
    )


def gather_normed(values):
    return lax.all_gather(values, "tensor", axis=0, tiled=True)


def gather_grads(values):
    return lax.all_gather(values, "tensor", axis=0, tiled=True)


def sum_branch(operand, weight):
    row_share = operand.shape[0] // lax.axis_size("tensor")

    def term(first_row, row_count):
        return dot_plain(operand, weight)

    return lax.psum_scatter(
        term(jnp.int32(0), row_share * lax.axis_size("tensor")).astype(jnp.bfloat16),
        "tensor",
        scatter_dimension=0,
        tiled=True,
    ).astype(jnp.float32)


def sum_inputs(grad_list, weight_list):
    row_share = grad_list[0].shape[0] // lax.axis_size("tensor")

    def term(first_row, row_count):
        summed = jnp.zeros((row_count, weight_list[0].shape[0]), jnp.float32)
        for grad_part, weight in zip(grad_list, weight_list):
            summed = summed + dot_back(grad_part, weight)
        return summed

    return lax.psum_scatter(
        term(jnp.int32(0), row_share * lax.axis_size("tensor")).astype(jnp.bfloat16),
        "tensor",
        scatter_dimension=0,
        tiled=True,
    ).astype(jnp.float32)


def split_heads(values, seq_len):
    return values.reshape(values.shape[0] // seq_len, seq_len, values.shape[1] // HEAD, HEAD)


def softmax_probs(query_rows, key_rows, allowed, seq_len):
    scores = jnp.einsum(
        "gqhe,gkhe->ghqk",
        split_heads(query_rows, seq_len),
        split_heads(key_rows, seq_len),
        preferred_element_type=jnp.float32,
    ) * HEAD ** (-0.5)
    if allowed is not None:
        scores = jnp.where(allowed, scores, -1000000000.0)
    highest = jnp.max(scores, axis=-1, keepdims=True)
    weights = jnp.exp(scores - highest)
    return weights / jnp.sum(weights, axis=-1, keepdims=True)


def block_forward(inputs, index, params, allowed, seq_len):
    norm_gain, norm_shift, w_qkv, qv_bias, out_proj, fc_in, fc_in_bias, fc_out, res_bias = params
    normed = layer_norm(inputs, norm_gain[index, 0], norm_shift[index, 0]).astype(jnp.bfloat16)
    gathered = gather_normed(normed)
    query_rows = (dot_plain(gathered, w_qkv[index, 0]) + qv_bias[index, 0]).astype(jnp.bfloat16)
    key_rows = dot_plain(gathered, w_qkv[index, 1]).astype(jnp.bfloat16)
    value_rows = (dot_plain(gathered, w_qkv[index, 2]) + qv_bias[index, 1]).astype(jnp.bfloat16)
    probs = softmax_probs(query_rows, key_rows, allowed, seq_len)
    mixed_heads = jnp.einsum(
        "ghqk,gkhe->gqhe",
        probs.astype(jnp.bfloat16),
        split_heads(value_rows, seq_len),
        preferred_element_type=jnp.float32,
    )
    mixed = mixed_heads.reshape(query_rows.shape).astype(jnp.bfloat16)
    middle = inputs + sum_branch(mixed, out_proj[index]) + res_bias[index, 0]
    normed_two = layer_norm(middle, norm_gain[index, 1], norm_shift[index, 1]).astype(jnp.bfloat16)
    gathered_two = gather_normed(normed_two)
    hidden = dot_plain(gathered_two, fc_in[index]) + fc_in_bias[index]
    active = (hidden * jax.nn.sigmoid(1.702 * hidden)).astype(jnp.bfloat16)
    output = middle + sum_branch(active, fc_out[index]) + res_bias[index, 1]
    saved = (
        inputs,
        gathered,
        query_rows,
        key_rows,
        value_rows,
        probs,
        mixed,
        middle,
        gathered_two,
        hidden,
        active,
    )
    return (output, saved)


def block_backward(grad_out, index, params, saved, seq_len, orders):
    norm_gain, norm_shift, w_qkv, qv_bias, out_proj, fc_in, fc_in_bias, fc_out, res_bias = params
    (
        inputs,
        gathered,
        query_rows,
        key_rows,
        value_rows,
        probs,
        mixed,
        middle,
        gathered_two,
        hidden,
        active,
    ) = saved
    grad_res_two = jnp.sum(grad_out, axis=0)
    grad_branch_two = gather_grads(grad_out.astype(jnp.bfloat16))
    grad_active = dot_back(grad_branch_two, fc_out[index])
    sigma = jax.nn.sigmoid(1.702 * hidden)
    grad_hidden = (grad_active * (sigma + 1.702 * hidden * sigma * (1.0 - sigma))).astype(
        jnp.bfloat16
    )
    grad_fc_in_bias = jnp.sum(grad_hidden, axis=0, dtype=jnp.float32)
    grad_normed_two = sum_inputs((grad_hidden,), (fc_in[index],))
    pull_two = jax.vjp(layer_norm, middle, norm_gain[index, 1], norm_shift[index, 1])[1]
    grad_middle_part, grad_gain_two, grad_shift_two = pull_two(grad_normed_two)
    grad_middle = grad_out + grad_middle_part
    grad_res_one = jnp.sum(grad_middle, axis=0)
    grad_branch_one = gather_grads(grad_middle.astype(jnp.bfloat16))
    grad_fc_out, grad_out_proj = sum_matrices(
        [(grad_branch_two, active), (grad_branch_one, mixed)], orders[0]
    )
    grad_fc_out, grad_out_proj = grad_fc_out.T, grad_out_proj.T
    grad_mixed = dot_back(grad_branch_one, out_proj[index]).astype(jnp.bfloat16)
    query_heads = split_heads(query_rows, seq_len)
    key_heads = split_heads(key_rows, seq_len)
    value_heads = split_heads(value_rows, seq_len)
    grad_heads = split_heads(grad_mixed, seq_len)
    grad_probs = jnp.einsum(
        "gqhe,gkhe->ghqk", grad_heads, value_heads, preferred_element_type=jnp.float32
    )
    grad_value = jnp.einsum(
        "ghqk,gqhe->gkhe",
        probs.astype(jnp.bfloat16),
        grad_heads,
        preferred_element_type=jnp.float32,
    )
    grad_value = grad_value.reshape(value_rows.shape).astype(jnp.bfloat16)
    grad_scores = (
        probs * (grad_probs - jnp.sum(probs * grad_probs, axis=-1, keepdims=True))
    ).astype(jnp.bfloat16)
    grad_query = jnp.einsum(
        "ghqk,gkhe->gqhe", grad_scores, key_heads, preferred_element_type=jnp.float32
    ) * HEAD ** (-0.5)
    grad_query = grad_query.reshape(query_rows.shape).astype(jnp.bfloat16)
    grad_key = jnp.einsum(
        "ghqk,gqhe->gkhe", grad_scores, query_heads, preferred_element_type=jnp.float32
    ) * HEAD ** (-0.5)
    grad_key = grad_key.reshape(key_rows.shape).astype(jnp.bfloat16)
    grad_qv_bias = jnp.stack(
        [
            jnp.sum(grad_query, axis=0, dtype=jnp.float32),
            jnp.sum(grad_value, axis=0, dtype=jnp.float32),
        ]
    )
    grad_fc_in, grad_query_w, grad_key_w, grad_value_w = sum_matrices(
        [
            (gathered_two, grad_hidden),
            (gathered, grad_query),
            (gathered, grad_key),
            (gathered, grad_value),
        ],
        orders[1],
    )
    grad_qkv = jnp.stack([grad_query_w, grad_key_w, grad_value_w])
    grad_normed = sum_inputs(
        (grad_query, grad_key, grad_value), (w_qkv[index, 0], w_qkv[index, 1], w_qkv[index, 2])
    )
    pull_one = jax.vjp(layer_norm, inputs, norm_gain[index, 0], norm_shift[index, 0])[1]
    grad_inputs_part, grad_gain_one, grad_shift_one = pull_one(grad_normed)
    grad_inputs = grad_middle + grad_inputs_part
    layer_grads = (
        jnp.stack([grad_gain_one, grad_gain_two]),
        jnp.stack([grad_shift_one, grad_shift_two]),
        grad_qkv,
        grad_qv_bias,
        grad_out_proj,
        grad_fc_in,
        grad_fc_in_bias,
        grad_fc_out,
        jnp.stack([grad_res_one, grad_res_two]),
    )
    return (grad_inputs, layer_grads)


def dp_bits():
    return (lax.axis_size("dp") - 1).bit_length()


def slice_order(order):
    me = lax.axis_index("dp")
    places = jnp.arange(lax.axis_size("dp"))
    source = jnp.zeros_like(places)
    for digit, bit in enumerate(order):
        source = source | (((places >> (len(order) - 1 - digit)) & 1) << bit)
    return source ^ me


def pick_matrix(width, order):
    depth = width // lax.axis_size("dp")
    wanted = jnp.repeat(slice_order(order) * depth, depth) + jnp.tile(
        jnp.arange(depth), lax.axis_size("dp")
    )
    return (jnp.arange(width)[:, None] == wanted[None, :]).astype(jnp.bfloat16)


def swap(values, bit):
    size = lax.axis_size("dp")
    return lax.ppermute(values, "dp", [(spot, spot ^ (1 << bit)) for spot in range(size)])


def sum_matrices(pairs, order):
    picks = pick_matrix(pairs[0][0].shape[1], order)
    terms = [
        dot_over(dot_plain(left, picks).astype(jnp.bfloat16), right) for left, right in pairs
    ]
    total = jnp.concatenate(terms, axis=1)
    for bit in order:
        half = total.shape[0] // 2
        total = total[:half] + swap(total[half:].astype(jnp.bfloat16), bit).astype(jnp.float32)
    cuts = []
    first = 0
    for _, right in pairs:
        cuts.append(total[:, first : first + right.shape[1]])
        first += right.shape[1]
    return cuts


def sum_small(members):
    flat = jnp.concatenate([member.reshape(-1) for member in members])
    flat = flat + lax.ppermute(flat, "tensor", [(0, 1), (1, 0)])
    for bit in range(dp_bits()):
        flat = flat + swap(flat, bit)
    parts = []
    first = 0
    for member in members:
        parts.append(flat[first : first + member.size].reshape(member.shape))
        first += member.size
    return parts


def run_tower(inputs, params, cotangent, allowed, seq_len, orders):
    depth_count = params[0].shape[0]
    kept = []
    state = inputs.astype(jnp.float32)
    for index in range(depth_count):
        state, saved = block_forward(state, index, params, allowed, seq_len)
        kept.append(saved)
    grad_state = cotangent
    collected = []
    for index in reversed(range(depth_count)):
        grad_state, layer_grads = block_backward(
            grad_state, index, params, kept[index], seq_len, orders[index]
        )
        collected.insert(0, layer_grads)
    stacked = tuple((jnp.stack([entry[member] for entry in collected]) for member in range(9)))
    return (state, grad_state, stacked)


def widen(values, full_width):
    placed = jnp.zeros(values.shape[:-1] + (full_width,), jnp.float32)
    return lax.dynamic_update_slice_in_dim(
        placed, values, lax.axis_index("tensor") * values.shape[-1], values.ndim - 1
    )


def on_device(
    image_in,
    image_norm_gain,
    image_norm_shift,
    image_qkv,
    image_qv_bias,
    image_out_proj,
    image_fc_in,
    image_fc_in_bias,
    image_fc_out,
    image_res_bias,
    image_cot,
    caption_in,
    caption_norm_gain,
    caption_norm_shift,
    caption_qkv,
    caption_qv_bias,
    caption_out_proj,
    caption_fc_in,
    caption_fc_in_bias,
    caption_fc_out,
    caption_res_bias,
    caption_lengths,
    caption_cot,
):
    image_params = (
        image_norm_gain,
        image_norm_shift,
        image_qkv,
        image_qv_bias,
        image_out_proj,
        image_fc_in,
        image_fc_in_bias,
        image_fc_out,
        image_res_bias,
    )
    caption_params = (
        caption_norm_gain,
        caption_norm_shift,
        caption_qkv,
        caption_qv_bias,
        caption_out_proj,
        caption_fc_in,
        caption_fc_in_bias,
        caption_fc_out,
        caption_res_bias,
    )
    spots = jnp.arange(CTX)
    caption_mask = (spots[None, None, None, :] <= spots[None, None, :, None]) & (
        spots[None, None, None, :] < caption_lengths[:, None, None, None]
    )
    bits = list(range(dp_bits()))
    first_way, second_way = bits, [1, 0] + bits[2:]
    orders = [(first_way, second_way), (second_way, first_way)]
    caption_out, caption_grad, caption_grads = run_tower(
        caption_in, caption_params, caption_cot, caption_mask, CTX, orders
    )
    image_out, image_grad, image_grads = run_tower(
        image_in, image_params, image_cot, None, PATCHES, orders
    )
    summed = [image_grads[member] for member in (2, 4, 5, 7)]
    summed += [caption_grads[member] for member in (2, 4, 5, 7)]
    small = sum_small(
        (
            image_grads[0],
            image_grads[1],
            widen(image_grads[3], DI),
            widen(image_grads[6], FI),
            image_grads[8],
            caption_grads[0],
            caption_grads[1],
            widen(caption_grads[3], DT),
            widen(caption_grads[6], FT),
            caption_grads[8],
        )
    )
    return (
        image_out,
        image_grad,
        small[0],
        small[1],
        summed[0],
        small[2],
        summed[1],
        summed[2],
        small[3],
        summed[3],
        small[4],
        caption_out,
        caption_grad,
        small[5],
        small[6],
        summed[4],
        small[7],
        summed[5],
        summed[6],
        small[8],
        summed[7],
        small[9],
    )


def solution(mesh):
    placed = (
        P(("dp", "tensor"), None),
        P(),
        P(),
        P(None, None, None, "tensor"),
        P(None, None, "tensor"),
        P(None, "tensor", None),
        P(None, None, "tensor"),
        P(None, "tensor"),
        P(None, "tensor", None),
        P(),
        P(("dp", "tensor"), None),
        P(("dp", "tensor"), None),
        P(),
        P(),
        P(None, None, None, "tensor"),
        P(None, None, "tensor"),
        P(None, "tensor", None),
        P(None, None, "tensor"),
        P(None, "tensor"),
        P(None, "tensor", None),
        P(),
        P("dp"),
        P(("dp", "tensor"), None),
    )
    return jax.shard_map(
        on_device,
        mesh=mesh,
        in_specs=placed,
        out_specs=(
            P(("dp", "tensor"), None),
            P(("dp", "tensor"), None),
            P(),
            P(),
            P(None, None, "dp", "tensor"),
            P(),
            P(None, "tensor", "dp"),
            P(None, "dp", "tensor"),
            P(),
            P(None, "tensor", "dp"),
            P(),
            P(("dp", "tensor"), None),
            P(("dp", "tensor"), None),
            P(),
            P(),
            P(None, None, "dp", "tensor"),
            P(),
            P(None, "tensor", "dp"),
            P(None, "dp", "tensor"),
            P(),
            P(None, "tensor", "dp"),
            P(),
        ),
        check_vma=False,
    )
```

```python
import functools

import jax
import jax.numpy as jnp
from jax import lax
from jax.experimental import pallas as pl
from jax.experimental.pallas import tpu as pltpu
from jax.sharding import PartitionSpec as P

HEAD = 64
PATCHES = 50
CTX = 77
EPS = 1e-05
SCALE = HEAD ** (-0.5)
LOW = jnp.bfloat16
WIDE = jnp.float32
ROOM = 56 * 1024 * 1024


def dot_plain(first, second):
    return jnp.dot(first, second, preferred_element_type=WIDE)


def dot_back(first, second):
    return lax.dot_general(first, second, (((1,), (1,)), ((), ())), preferred_element_type=WIDE)


def dot_over(first, second):
    return lax.dot_general(first, second, (((0,), (0,)), ((), ())), preferred_element_type=WIDE)


def spread_of(values):
    centred = values - jnp.mean(values, axis=-1, keepdims=True)
    inverse = lax.rsqrt(jnp.mean(centred * centred, axis=-1, keepdims=True) + EPS)
    return centred * inverse, inverse


def norm_back(grad, unit, inverse, gain):
    scaled = grad * gain
    return inverse * (
        scaled
        - jnp.mean(scaled, axis=-1, keepdims=True)
        - unit * jnp.mean(scaled * unit, axis=-1, keepdims=True)
    )


def column_sum(values):
    return jnp.sum(values.astype(WIDE), axis=0, keepdims=True)


def allowed_keys(rows, length):
    query = lax.broadcasted_iota(jnp.int32, (rows, rows), 0)
    key = lax.broadcasted_iota(jnp.int32, (rows, rows), 1)
    if length is None:
        return (query // PATCHES) == (key // PATCHES)
    return (key <= query) & (key < length)


def store_left(values, member, places, turned, keep, send):
    turned[...] = values.astype(WIDE).T.astype(LOW)
    count = places.shape[0]
    depth = turned.shape[0] // count
    if depth % 16:
        half = turned.shape[0] // 2
        keep[member] = turned[:half]
        send[member] = turned[half:]
        return
    for spot in range(count):
        block = turned[pl.ds(pl.multiple_of(places[spot] * depth, depth), depth), :]
        if spot < count // 2:
            keep[member, spot * depth : (spot + 1) * depth, :] = block
        else:
            first = (spot - count // 2) * depth
            send[member, first : first + depth, :] = block


def pull_in(index, sources, targets, sems):
    copies = []
    for spot, (source, target) in enumerate(zip(sources, targets)):
        copy = pltpu.make_async_copy(source.at[index], target, sems.at[spot])
        copy.start()
        copies.append(copy)
    return copies


def forward_kernel(index, causal, places, length, *refs):
    (
        inputs, gain, shift, res_bias, qv_own, qv_far, fcb_own, fcb_far,
        wq_own, wq_far, wo_own, wo_far, wi_own, wi_far, wf_own, wf_far,
        output, heads_out, probs_out, middle_out, hidden_out, right_out, keep_out, send_out,
        wq0, wq1, wo0, wo1, wi0, wi1, wf0, wf1, turned, sems,
    ) = refs
    copies = pull_in(
        index,
        (wq_own, wq_far, wo_own, wo_far, wi_own, wi_far, wf_own, wf_far),
        (wq0, wq1, wo0, wo1, wi0, wi1, wf0, wf1),
        sems,
    )
    rows, width = inputs.shape
    part = width // 2
    units = wi0.shape[1]
    state = inputs[...].astype(WIDE)
    unit, _ = spread_of(state)
    normed = (unit * gain[index, 0:1] + shift[index, 0:1]).astype(LOW)
    store_left(normed, 1, places, turned, keep_out, send_out)
    mask = allowed_keys(rows, length[0] if causal else None)
    lane = lax.broadcasted_iota(jnp.int32, (rows, 128), 1)
    first_head = lane < HEAD
    for side, (wq, bias) in enumerate(((wq0, qv_own), (wq1, qv_far))):
        copies[side].wait()
        heads_out[side, 0] = (dot_plain(normed, wq[0]) + bias[index, 0:1]).astype(LOW)
        heads_out[side, 1] = dot_plain(normed, wq[1]).astype(LOW)
        heads_out[side, 2] = (dot_plain(normed, wq[2]) + bias[index, 1:2]).astype(LOW)
    for side in range(2):
        for pair in range(part // 128):
            cols = slice(pair * 128, pair * 128 + 128)
            query = heads_out[side, 0, :, cols]
            key = heads_out[side, 1, :, cols]
            value = heads_out[side, 2, :, cols]
            mixed = []
            for which in range(2):
                chosen = first_head if which == 0 else ~first_head
                scores = dot_back(jnp.where(chosen, query, jnp.zeros_like(query)), key) * SCALE
                scores = jnp.where(mask, scores, -1000000000.0)
                weights = jnp.exp(scores - jnp.max(scores, axis=-1, keepdims=True))
                probs = weights / jnp.sum(weights, axis=-1, keepdims=True)
                probs_out[(side * (part // 128) + pair) * 2 + which] = probs
                mixed.append(dot_plain(probs.astype(LOW), value))
            right_out[side, :, units + pair * 128 : units + pair * 128 + 128] = jnp.where(
                first_head, mixed[0], mixed[1]
            ).astype(LOW)
    middle = state + res_bias[index, 0:1]
    for side, wo in enumerate((wo0, wo1)):
        copies[2 + side].wait()
        middle = middle + dot_plain(right_out[side, :, units : units + part], wo[...])
    middle_out[...] = middle
    unit, _ = spread_of(middle)
    normed_two = (unit * gain[index, 1:2] + shift[index, 1:2]).astype(LOW)
    store_left(normed_two, 0, places, turned, keep_out, send_out)
    total = middle + res_bias[index, 1:2]
    for side, (wi, wf, bias) in enumerate(((wi0, wf0, fcb_own), (wi1, wf1, fcb_far))):
        copies[4 + side].wait()
        hidden = dot_plain(normed_two, wi[...]) + bias[index : index + 1]
        hidden_out[side] = hidden
        active = (hidden * jax.nn.sigmoid(1.702 * hidden)).astype(LOW)
        right_out[side, :, 0:units] = active
        copies[6 + side].wait()
        total = total + dot_plain(active, wf[...])
    output[...] = total


def backward_kernel(index, places, *refs):
    (
        grad_in, inputs, middle, hidden_in, heads, probs_in, gain,
        wf_own, wf_far, wi_own, wi_far, wo_own, wo_far, wq_own, wq_far,
        grad_out, right_out, small_out, keep_out, send_out,
        wf0, wf1, wi0, wi1, wo0, wo1, wq0, wq1, turned, sems,
    ) = refs
    copies = pull_in(
        index,
        (wf_own, wf_far, wi_own, wi_far, wo_own, wo_far, wq_own, wq_far),
        (wf0, wf1, wi0, wi1, wo0, wo1, wq0, wq1),
        sems,
    )
    rows, width = inputs.shape
    part = width // 2
    units = wi0.shape[1]
    per_row = units // width
    grad = grad_in[...]
    small_out[11:12] = column_sum(grad)
    branch_two = grad.astype(LOW)
    store_left(branch_two, 0, places, turned, keep_out, send_out)
    grad_normed = jnp.zeros((rows, width), WIDE)
    for side, (wf, wi) in enumerate(((wf0, wi0), (wf1, wi1))):
        copies[side].wait()
        grad_active = dot_back(branch_two, wf[...])
        hidden = hidden_in[side]
        sigma = jax.nn.sigmoid(1.702 * hidden)
        grad_hidden = (
            grad_active * (sigma + 1.702 * hidden * sigma * (1.0 - sigma))
        ).astype(LOW)
        right_out[side, :, 0:units] = grad_hidden
        sums = column_sum(grad_hidden)
        for row in range(per_row):
            small_out[6 + side * per_row + row : 7 + side * per_row + row] = sums[
                :, row * width : (row + 1) * width
            ]
        copies[2 + side].wait()
        grad_normed = grad_normed + dot_back(grad_hidden, wi[...])
    unit, inverse = spread_of(middle[...])
    small_out[1:2] = column_sum(grad_normed * unit)
    small_out[3:4] = column_sum(grad_normed)
    grad_middle = grad + norm_back(grad_normed, unit, inverse, gain[index, 1:2])
    small_out[10:11] = column_sum(grad_middle)
    branch_one = grad_middle.astype(LOW)
    store_left(branch_one, 1, places, turned, keep_out, send_out)
    lane = lax.broadcasted_iota(jnp.int32, (rows, 128), 1)
    first_head = lane < HEAD
    grad_normed = jnp.zeros((rows, width), WIDE)
    for side, wo in enumerate((wo0, wo1)):
        copies[4 + side].wait()
        grad_mixed = dot_back(branch_one, wo[...]).astype(LOW)
        for pair in range(part // 128):
            cols = slice(pair * 128, pair * 128 + 128)
            query = heads[side, 0, :, cols]
            key = heads[side, 1, :, cols]
            value = heads[side, 2, :, cols]
            mixed = grad_mixed[:, cols]
            found = []
            for which in range(2):
                chosen = first_head if which == 0 else ~first_head
                probs = probs_in[(side * (part // 128) + pair) * 2 + which]
                grad_probs = dot_back(jnp.where(chosen, mixed, jnp.zeros_like(mixed)), value)
                grad_value = dot_over(probs.astype(LOW), mixed)
                shared = jnp.sum(probs * grad_probs, axis=-1, keepdims=True)
                grad_scores = (probs * (grad_probs - shared)).astype(LOW)
                found.append(
                    (
                        dot_plain(grad_scores, key) * SCALE,
                        dot_over(grad_scores, query) * SCALE,
                        grad_value,
                    )
                )
            for member in range(3):
                first = units + member * part + pair * 128
                right_out[side, :, first : first + 128] = jnp.where(
                    first_head, found[0][member], found[1][member]
                ).astype(LOW)
    for side, wq in enumerate((wq0, wq1)):
        copies[6 + side].wait()
        for member in range(3):
            first = units + member * part
            piece = right_out[side, :, first : first + part]
            if member != 1:
                small_out[4 + member // 2 : 5 + member // 2, side * part : (side + 1) * part] = (
                    column_sum(piece)
                )
            grad_normed = grad_normed + dot_back(piece, wq[member])
    unit, inverse = spread_of(inputs[...].astype(WIDE))
    small_out[0:1] = column_sum(grad_normed * unit)
    small_out[2:3] = column_sum(grad_normed)
    grad_out[...] = grad_middle + norm_back(grad_normed, unit, inverse, gain[index, 0:1])


IN_VMEM = pl.BlockSpec(memory_space=pltpu.VMEM)
IN_SMEM = pl.BlockSpec(memory_space=pltpu.SMEM)
ANYWHERE = pl.BlockSpec(memory_space=pl.ANY)


def shape_of(dims, kind):
    return jax.ShapeDtypeStruct(dims, kind)


def run_forward(state, index, params, places, length):
    gain, shift, res_bias, own, far = params
    rows, width = state.shape
    part = width // 2
    units = own[3].shape[2]
    heads = width // HEAD
    half = width // 2
    weights = [own[0], far[0], own[2], far[2], own[3], far[3], own[5], far[5]]
    biases = [own[1], far[1], own[4], far[4]]
    causal = length is not None
    args = [places, length if causal else places]
    args += [state, gain, shift, res_bias] + biases + weights
    return pl.pallas_call(
        functools.partial(forward_kernel, index, causal),
        in_specs=[IN_SMEM] * 2 + [IN_VMEM] * 8 + [ANYWHERE] * 8,
        out_specs=[IN_VMEM] * 8,
        out_shape=[
            shape_of((rows, width), WIDE),
            shape_of((2, 3, rows, part), LOW),
            shape_of((heads, rows, rows), WIDE),
            shape_of((rows, width), WIDE),
            shape_of((2, rows, units), WIDE),
            shape_of((2, rows, units + part), LOW),
            shape_of((2, half, rows), LOW),
            shape_of((2, half, rows), LOW),
        ],
        scratch_shapes=[pltpu.VMEM(w.shape[1:], LOW) for w in weights]
        + [pltpu.VMEM((width, rows), LOW), pltpu.SemaphoreType.DMA((8,))],
        compiler_params=pltpu.CompilerParams(vmem_limit_bytes=ROOM),
        cost_estimate=pl.CostEstimate(
            flops=24 * rows * width * width,
            bytes_accessed=24 * width * width,
            transcendentals=4 * rows * width,
        ),
    )(*args)


def run_backward(grad, state, index, params, kept, places):
    gain, _, _, own, far = params
    _, heads, probs, middle, hidden = kept
    rows, width = state.shape
    part = width // 2
    units = own[3].shape[2]
    half = width // 2
    weights = [own[5], far[5], own[3], far[3], own[2], far[2], own[0], far[0]]
    args = [places, grad, state, middle, hidden, heads, probs, gain] + weights
    return pl.pallas_call(
        functools.partial(backward_kernel, index),
        in_specs=[IN_SMEM] + [IN_VMEM] * 7 + [ANYWHERE] * 8,
        out_specs=[IN_VMEM] * 5,
        out_shape=[
            shape_of((rows, width), WIDE),
            shape_of((2, rows, units + 3 * part), LOW),
            shape_of((12, width), WIDE),
            shape_of((2, half, rows), LOW),
            shape_of((2, half, rows), LOW),
        ],
        scratch_shapes=[pltpu.VMEM(w.shape[1:], LOW) for w in weights]
        + [pltpu.VMEM((width, rows), LOW), pltpu.SemaphoreType.DMA((8,))],
        compiler_params=pltpu.CompilerParams(vmem_limit_bytes=ROOM),
        cost_estimate=pl.CostEstimate(
            flops=24 * rows * width * width,
            bytes_accessed=24 * width * width,
            transcendentals=4 * rows * width,
        ),
    )(*args)


def far_kernel(left, left_far, right, right_far, product):
    product[...] = (dot_plain(left[0], right[0]) + dot_plain(left_far[0], right_far[0])).astype(LOW)


def near_kernel(left, left_far, right, right_far, arrived, keep, send):
    total = dot_plain(left[0], right[0]) + dot_plain(left_far[0], right_far[0])
    total = total + arrived[...].astype(WIDE)
    half = total.shape[0] // 2
    keep[...] = total[:half]
    send[...] = total[half:].astype(LOW)


def run_product(left, left_far, right, right_far, arrived):
    _, half, rows = left.shape
    columns = right.shape[2]
    step = half
    fc_steps = 4
    side = 1 if arrived is None else 0
    lefts = pl.BlockSpec((1, half, rows), lambda j: (j // fc_steps, 0, 0))
    rights = pl.BlockSpec((1, rows, step), lambda j: (side, 0, j))
    whole = pl.BlockSpec((half, step), lambda j: (0, j))
    split = pl.BlockSpec((half // 2, step), lambda j: (0, j))
    in_specs = [lefts, lefts, rights, rights]
    args = [left, left_far, right, right_far]
    cost = pl.CostEstimate(
        flops=4 * half * rows * columns, bytes_accessed=4 * half * columns, transcendentals=0
    )
    if arrived is None:
        return pl.pallas_call(
            far_kernel,
            grid=(columns // step,),
            in_specs=in_specs,
            out_specs=whole,
            out_shape=shape_of((half, columns), LOW),
            cost_estimate=cost,
        )(*args)
    return pl.pallas_call(
        near_kernel,
        grid=(columns // step,),
        in_specs=in_specs + [whole],
        out_specs=[split, split],
        out_shape=[
            shape_of((half // 2, columns), WIDE),
            shape_of((half // 2, columns), LOW),
        ],
        cost_estimate=cost,
    )(*args, arrived)


def dp_bits():
    return (lax.axis_size("dp") - 1).bit_length()


def slice_order(order, relative):
    me = lax.axis_index("dp")
    places = jnp.arange(lax.axis_size("dp"), dtype=jnp.int32)
    source = jnp.zeros_like(places)
    for digit, bit in enumerate(order):
        value = (places >> (len(order) - 1 - digit)) & 1
        if digit < relative:
            value = value ^ ((me >> bit) & 1)
        source = source | (value << bit)
    return source


def swap(values, bit):
    size = lax.axis_size("dp")
    return lax.ppermute(values, "dp", [(spot, spot ^ (1 << bit)) for spot in range(size)])


def swap_cores(values):
    return lax.ppermute(values, "tensor", [(0, 1), (1, 0)])


def arrange(keep, send, places):
    count = places.shape[0]
    members, half, rows = keep.shape
    if (2 * half // count) % 16 == 0:
        return keep, send
    full = jnp.concatenate([keep, send], axis=1).reshape(members, count, -1, rows)
    full = jnp.take(full, places, axis=1).reshape(members, 2 * half, rows)
    return full[:, :half], full[:, half:]


def sum_group(left, left_far, right, right_far, order, relative):
    arrived = swap_cores(run_product(left, left_far, right, right_far, None))
    keep, send = run_product(left, left_far, right, right_far, arrived)
    total = keep + swap(send, order[1]).astype(WIDE)
    if relative == 2:
        size = lax.axis_size("dp")
        groups = [[spot for spot in range(size) if spot % 4 == low] for low in range(4)]
        return lax.psum_scatter(
            total.astype(LOW), "dp", scatter_dimension=0, tiled=True, axis_index_groups=groups
        ).astype(WIDE)
    for bit in order[2:]:
        half = total.shape[0] // 2
        total = total[:half] + swap(total[half:].astype(LOW), bit).astype(WIDE)
    return total


def sum_small(values):
    values = values + swap_cores(values)
    for bit in range(dp_bits()):
        values = values + swap(values, bit)
    return values


def run_tower(inputs, params, cotangent, length, ways):
    depth_count = params[0].shape[0]
    state = inputs
    states = []
    kept = []
    for index in range(depth_count):
        states.append(state)
        first, second = ways[index]
        places = slice_order(*second)
        state, heads, probs, middle, hidden, right, keep, send = run_forward(
            state, index, params, places, length
        )
        keep, send = arrange(keep, send, places)
        right_far = swap(right, first[0][0])
        left_far = swap(send, second[0][0])
        kept.append(
            ((state, heads, probs, middle, hidden), (right, right_far), (keep, left_far))
        )
    grad = cotangent
    sums = []
    smalls = []
    for index in reversed(range(depth_count)):
        first, second = ways[index]
        saved, rights, lefts = kept[index]
        places = slice_order(*first)
        grad, right, small, keep, send = run_backward(
            grad, states[index], index, params, saved, places
        )
        keep, send = arrange(keep, send, places)
        left_far = swap(send, first[0][0])
        right_far = swap(right, second[0][0])
        out_sum = sum_group(keep, left_far, rights[0], rights[1], *first)
        in_sum = sum_group(lefts[0], lefts[1], right, right_far, *second)
        sums.insert(0, (out_sum, in_sum))
        smalls.insert(0, small)
    return state, grad, sums, smalls


def matrix_grads(sums, width):
    part = width // 2
    qkv, out_proj, fc_in, fc_out = [], [], [], []
    for out_sum, in_sum in sums:
        units = out_sum.shape[1] - part
        fc_out.append(out_sum[:, :units].T)
        out_proj.append(out_sum[:, units:].T)
        fc_in.append(in_sum[:, :units])
        qkv.append(
            jnp.stack([in_sum[:, units + m * part : units + (m + 1) * part] for m in range(3)])
        )
    return [jnp.stack(member) for member in (qkv, out_proj, fc_in, fc_out)]


def small_grads(values, width):
    part = width // 2
    values = values.reshape(2, 12, width)
    gains = values[:, 0:2]
    shifts = values[:, 2:4]
    qv_bias = values[:, 4:6]
    fc_in_bias = values[:, 6:10].reshape(2, 4 * width)
    res_bias = values[:, 10:12]
    return gains, shifts, qv_bias, fc_in_bias, res_bias


def order_sides(values, width):
    part = width // 2
    swapped = jnp.concatenate(
        [
            values[:, 0:4],
            jnp.concatenate([values[:, 4:6, part:], values[:, 4:6, :part]], axis=2),
            values[:, 8:10],
            values[:, 6:8],
            values[:, 10:12],
        ],
        axis=1,
    )
    return jnp.where(lax.axis_index("tensor") == 0, values, swapped)


def on_device(
    image_in,
    image_norm_gain,
    image_norm_shift,
    image_qkv,
    image_qv_bias,
    image_out_proj,
    image_fc_in,
    image_fc_in_bias,
    image_fc_out,
    image_res_bias,
    image_cot,
    caption_in,
    caption_norm_gain,
    caption_norm_shift,
    caption_qkv,
    caption_qv_bias,
    caption_out_proj,
    caption_fc_in,
    caption_fc_in_bias,
    caption_fc_out,
    caption_res_bias,
    caption_lengths,
    caption_cot,
):
    image_own = (
        image_qkv,
        image_qv_bias,
        image_out_proj,
        image_fc_in,
        image_fc_in_bias,
        image_fc_out,
    )
    caption_own = (
        caption_qkv,
        caption_qv_bias,
        caption_out_proj,
        caption_fc_in,
        caption_fc_in_bias,
        caption_fc_out,
    )
    caption_far = tuple(swap_cores(member) for member in caption_own)
    image_far = tuple(swap_cores(member) for member in image_own)
    image_params = (image_norm_gain, image_norm_shift, image_res_bias, image_own, image_far)
    caption_params = (
        caption_norm_gain,
        caption_norm_shift,
        caption_res_bias,
        caption_own,
        caption_far,
    )
    count = dp_bits()
    upper = list(range(2, count))
    by_links = [([0, 1] + upper, count), ([1, 0] + upper, count)]
    by_sum = [([0, 1] + upper[::-1], 2), ([1, 0] + upper[::-1], 2)]
    length = lax.dynamic_slice_in_dim(caption_lengths, lax.axis_index("tensor"), 1)
    caption_out, caption_grad, caption_sums, caption_smalls = run_tower(
        caption_in,
        caption_params,
        caption_cot,
        length,
        [(by_sum[0], by_sum[1]), (by_sum[1], by_sum[0])],
    )
    image_out, image_grad, image_sums, image_smalls = run_tower(
        image_in,
        image_params,
        image_cot,
        None,
        [(by_links[0], by_links[1]), (by_links[1], by_links[0])],
    )
    image_width = image_in.shape[1]
    caption_width = caption_in.shape[1]
    image_flat = order_sides(jnp.stack(image_smalls), image_width).reshape(-1, 128)
    caption_flat = order_sides(jnp.stack(caption_smalls), caption_width).reshape(-1, 128)
    small = sum_small(jnp.concatenate([image_flat, caption_flat]))
    image_small = small_grads(small[: image_flat.shape[0]], image_width)
    caption_small = small_grads(small[image_flat.shape[0] :], caption_width)
    image_matrix = matrix_grads(image_sums, image_width)
    caption_matrix = matrix_grads(caption_sums, caption_width)
    outs = []
    for out, grad, few, matrix in (
        (image_out, image_grad, image_small, image_matrix),
        (caption_out, caption_grad, caption_small, caption_matrix),
    ):
        outs += [
            out,
            grad,
            few[0],
            few[1],
            matrix[0],
            few[2],
            matrix[1],
            matrix[2],
            few[3],
            matrix[3],
            few[4],
        ]
    return tuple(outs)


def solution(mesh):
    placed = (
        P(("dp", "tensor"), None),
        P(),
        P(),
        P(None, None, None, "tensor"),
        P(None, None, "tensor"),
        P(None, "tensor", None),
        P(None, None, "tensor"),
        P(None, "tensor"),
        P(None, "tensor", None),
        P(),
        P(("dp", "tensor"), None),
        P(("dp", "tensor"), None),
        P(),
        P(),
        P(None, None, None, "tensor"),
        P(None, None, "tensor"),
        P(None, "tensor", None),
        P(None, None, "tensor"),
        P(None, "tensor"),
        P(None, "tensor", None),
        P(),
        P("dp"),
        P(("dp", "tensor"), None),
    )
    return jax.shard_map(
        on_device,
        mesh=mesh,
        in_specs=placed,
        out_specs=(
            P(("dp", "tensor"), None),
            P(("dp", "tensor"), None),
            P(),
            P(),
            P(None, None, "dp", "tensor"),
            P(),
            P(None, "tensor", "dp"),
            P(None, "dp", "tensor"),
            P(),
            P(None, "tensor", "dp"),
            P(),
            P(("dp", "tensor"), None),
            P(("dp", "tensor"), None),
            P(),
            P(),
            P(None, None, "dp", "tensor"),
            P(),
            P(None, "tensor", "dp"),
            P(None, "dp", "tensor"),
            P(),
            P(None, "tensor", "dp"),
            P(),
        ),
        check_vma=False,
    )
```

```python
import functools

import jax
import jax.numpy as jnp
from jax import lax
from jax.experimental import pallas as pl
from jax.experimental.pallas import tpu as pltpu
from jax.sharding import PartitionSpec as P

HEAD = 64
PATCHES = 50
CTX = 77
EPS = 1e-05
SCALE = HEAD ** (-0.5)
LOW = jnp.bfloat16
WIDE = jnp.float32
MIB = 1024 * 1024
LANES = 128


def dot_plain(first, second):
    return jnp.dot(first, second, preferred_element_type=WIDE)


def dot_back(first, second):
    return lax.dot_general(first, second, (((1,), (1,)), ((), ())), preferred_element_type=WIDE)


def dot_over(first, second):
    return lax.dot_general(first, second, (((0,), (0,)), ((), ())), preferred_element_type=WIDE)


def room_for(rows):
    return -(-rows // 16) * 16


def spread_of(values):
    centred = values - jnp.mean(values, axis=-1, keepdims=True)
    inverse = lax.rsqrt(jnp.mean(centred * centred, axis=-1, keepdims=True) + EPS)
    return centred * inverse, inverse


def norm_back(grad, unit, inverse, gain):
    scaled = grad * gain
    return inverse * (
        scaled
        - jnp.mean(scaled, axis=-1, keepdims=True)
        - unit * jnp.mean(scaled * unit, axis=-1, keepdims=True)
    )


def column_sum(values):
    return jnp.sum(values.astype(WIDE), axis=0, keepdims=True)


def allowed_keys(rows, length):
    query = lax.broadcasted_iota(jnp.int32, (rows, rows), 0)
    key = lax.broadcasted_iota(jnp.int32, (rows, rows), 1)
    if length is None:
        return (query // PATCHES) == (key // PATCHES)
    return (key <= query) & (key < length)


def with_room(source, held):
    held[...] = jnp.zeros_like(held)
    held[0 : source.shape[0], :] = source[...].astype(WIDE)
    return held[...]


def store_left(values, member, places, turned, sorted_rows, keep, send, send_base):
    rows, width = values.shape
    wide = values.astype(WIDE)
    if rows < LANES:
        wide = jnp.concatenate([wide, jnp.zeros((LANES - rows, width), WIDE)], axis=0)
    turned[...] = wide.T
    count = places.shape[0]
    depth = width // count
    half = width // 2
    if depth % 16:

        def move(row, carry):
            source = places[row // depth] * depth + row % depth
            sorted_rows[pl.ds(row, 1), :] = turned[pl.ds(source, 1), :]
            return carry

        lax.fori_loop(0, width, move, 0)
        keep[member * half : (member + 1) * half, :] = sorted_rows[0:half, :].astype(LOW)
        first = send_base + member * half
        send[first : first + half, :] = sorted_rows[half:width, :].astype(LOW)
        return
    for spot in range(count):
        block = turned[pl.ds(pl.multiple_of(places[spot] * depth, depth), depth), :].astype(LOW)
        if spot < count // 2:
            first = member * half + spot * depth
            keep[first : first + depth, :] = block
        else:
            first = send_base + member * half + spot * depth - half
            send[first : first + depth, :] = block


def store_chunks(values, target, first_chunk):
    rows = values.shape[0]
    for chunk in range(values.shape[1] // LANES):
        first = (first_chunk + chunk) * rows
        target[first : first + rows, :] = values[:, chunk * LANES : (chunk + 1) * LANES]


def pull_in(index, sources, targets, sems):
    copies = []
    for spot, (source, target) in enumerate(zip(sources, targets)):
        copy = pltpu.make_async_copy(source.at[index], target, sems.at[spot])
        copy.start()
        copies.append(copy)
    return copies


def forward_kernel(index, causal, bias_at, places, length, *refs):
    (
        inputs, gain, shift, res_bias, bias_own, bias_far,
        wq_own, wq_far, wo_own, wo_far, wi_own, wi_far, wf_own, wf_far,
        output, heads_out, probs_out, middle_out, hidden_out, right_out, keep_out, send_out,
        wq0, wq1, wo0, wo1, wi0, wi1, wf0, wf1, turned, sorted_rows, held, sems,
    ) = refs
    copies = pull_in(
        index,
        (wq_own, wq_far, wo_own, wo_far, wi_own, wi_far, wf_own, wf_far),
        (wq0, wq1, wo0, wo1, wi0, wi1, wf0, wf1),
        sems,
    )
    state = with_room(inputs, held)
    rows, width = state.shape
    part = width // 2
    units = wi0.shape[1]
    fc_chunks = units // LANES
    side_chunks = fc_chunks + part // LANES
    unit, _ = spread_of(state)
    normed = (unit * gain[index, 0:1] + shift[index, 0:1]).astype(LOW)
    store_left(normed, 1, places, turned, sorted_rows, keep_out, send_out, 0)
    mask = allowed_keys(rows, length[0] if causal else None)
    lane = lax.broadcasted_iota(jnp.int32, (rows, LANES), 1)
    first_head = lane < HEAD
    row = slice(index, index + 1)
    for side, (wq, bias) in enumerate(((wq0, bias_own), (wq1, bias_far))):
        copies[side].wait()
        first = bias[row, bias_at : bias_at + part]
        second = bias[row, bias_at + part : bias_at + width]
        heads_out[side, 0] = (dot_plain(normed, wq[0]) + first).astype(LOW)
        heads_out[side, 1] = dot_plain(normed, wq[1]).astype(LOW)
        heads_out[side, 2] = (dot_plain(normed, wq[2]) + second).astype(LOW)
    middle = state + res_bias[index, 0:1]
    for side, wo in enumerate((wo0, wo1)):
        pieces = []
        for pair in range(part // LANES):
            cols = slice(pair * LANES, (pair + 1) * LANES)
            query = heads_out[side, 0, :, cols]
            key = heads_out[side, 1, :, cols]
            value = heads_out[side, 2, :, cols]
            mixed = []
            for which in range(2):
                chosen = first_head if which == 0 else ~first_head
                scores = dot_back(jnp.where(chosen, query, jnp.zeros_like(query)), key) * SCALE
                scores = jnp.where(mask, scores, -1000000000.0)
                weights = jnp.exp(scores - jnp.max(scores, axis=-1, keepdims=True))
                probs = weights / jnp.sum(weights, axis=-1, keepdims=True)
                probs_out[(side * (part // LANES) + pair) * 2 + which] = probs
                mixed.append(dot_plain(probs.astype(LOW), value))
            pieces.append(jnp.where(first_head, mixed[0], mixed[1]).astype(LOW))
        mixed_rows = jnp.concatenate(pieces, axis=1)
        store_chunks(mixed_rows, right_out, side * side_chunks + fc_chunks)
        copies[2 + side].wait()
        middle = middle + dot_plain(mixed_rows, wo[...])
    middle_out[...] = middle
    unit, _ = spread_of(middle)
    normed_two = (unit * gain[index, 1:2] + shift[index, 1:2]).astype(LOW)
    store_left(normed_two, 0, places, turned, sorted_rows, keep_out, send_out, 0)
    total = middle + res_bias[index, 1:2]
    for side, (wi, wf, bias) in enumerate(((wi0, wf0, bias_own), (wi1, wf1, bias_far))):
        copies[4 + side].wait()
        first = bias_at + width
        hidden = dot_plain(normed_two, wi[...]) + bias[row, first : first + units]
        hidden_out[side] = hidden
        active = (hidden * jax.nn.sigmoid(1.702 * hidden)).astype(LOW)
        store_chunks(active, right_out, side * side_chunks)
        copies[6 + side].wait()
        total = total + dot_plain(active, wf[...])
    output[...] = total[0 : output.shape[0]]


def small_store(small, group, values):
    count = values.shape[1] // LANES
    for chunk in range(count):
        row = group + chunk
        small[row : row + 1, :] = values[:, chunk * LANES : (chunk + 1) * LANES]


def backward_kernel(index, layout, places, core, *refs):
    (
        grad_in, inputs, middle, hidden_in, heads, probs_in, gain,
        right_in, send_in, wf_own, wf_far, wi_own, wi_far, wo_own, wo_far, wq_own, wq_far,
    ) = refs[:17]
    grad_out, small_out, keep_out = refs[17:20]
    late = [spot for spot, parcel in enumerate(layout.parcels) if not parcel[0]]
    parcels = dict(zip(late, refs[20 : 20 + len(late)]))
    (
        wf0, wf1, wi0, wi1, wo0, wo1, wq0, wq1, turned, sorted_rows, held, sems, more_sems,
    ) = refs[20 + len(late) :]
    copies = pull_in(
        index,
        (wf_own, wf_far, wi_own, wi_far, wo_own, wo_far, wq_own, wq_far),
        (wf0, wf1, wi0, wi1, wo0, wo1, wq0, wq1),
        sems,
    )
    rows = layout.rows
    width = layout.width
    part = width // 2
    units = layout.units
    extra = []
    for item, source in ((("right", 0), right_in), (("left", 1), send_in)):
        spot, base = layout.place(item)
        if spot in parcels:
            extra.append(
                pltpu.make_async_copy(
                    source,
                    parcels[spot].at[pl.ds(base, layout.item_rows(item))],
                    more_sems.at[len(extra)],
                )
            )
    out_spot, out_base = layout.place(("left", 0))
    out_buffer = parcels[out_spot]
    in_spot, in_base = layout.place(("right", 1))
    in_buffer = parcels[in_spot]
    in_first = (in_base // rows, in_base // rows + layout.group_chunks[1])
    for copy in extra:
        copy.start()
    is_first = core[0] == 0
    grad = with_room(grad_in, held)
    per = width // LANES
    small_store(small_out, 11 * per, column_sum(grad))
    branch_two = grad.astype(LOW)
    store_left(
        branch_two, 0, places, turned, sorted_rows, keep_out, out_buffer, out_base
    )
    grad_normed = jnp.zeros((rows, width), WIDE)
    sums = []
    for side, (wf, wi) in enumerate(((wf0, wi0), (wf1, wi1))):
        copies[side].wait()
        grad_active = dot_back(branch_two, wf[...])
        hidden = hidden_in[side]
        sigma = jax.nn.sigmoid(1.702 * hidden)
        grad_hidden = (
            grad_active * (sigma + 1.702 * hidden * sigma * (1.0 - sigma))
        ).astype(LOW)
        store_chunks(grad_hidden, in_buffer, in_first[side])
        sums.append(column_sum(grad_hidden))
        copies[2 + side].wait()
        grad_normed = grad_normed + dot_back(grad_hidden, wi[...])
    small_store(small_out, 6 * per, jnp.where(is_first, sums[0], sums[1]))
    small_store(small_out, 8 * per, jnp.where(is_first, sums[1], sums[0]))
    unit, inverse = spread_of(middle[...])
    small_store(small_out, per, column_sum(grad_normed * unit))
    small_store(small_out, 3 * per, column_sum(grad_normed))
    grad_middle = grad + norm_back(grad_normed, unit, inverse, gain[index, 1:2])
    small_store(small_out, 10 * per, column_sum(grad_middle))
    branch_one = grad_middle.astype(LOW)
    store_left(
        branch_one, 1, places, turned, sorted_rows, keep_out, out_buffer, out_base
    )
    lane = lax.broadcasted_iota(jnp.int32, (rows, LANES), 1)
    first_head = lane < HEAD
    grad_normed = jnp.zeros((rows, width), WIDE)
    sums = []
    for side, (wo, wq) in enumerate(((wo0, wq0), (wo1, wq1))):
        copies[4 + side].wait()
        grad_mixed = dot_back(branch_one, wo[...]).astype(LOW)
        pieces = [[], [], []]
        for pair in range(part // LANES):
            cols = slice(pair * LANES, (pair + 1) * LANES)
            query = heads[side, 0, :, cols]
            key = heads[side, 1, :, cols]
            value = heads[side, 2, :, cols]
            mixed = grad_mixed[:, cols]
            found = []
            for which in range(2):
                chosen = first_head if which == 0 else ~first_head
                probs = probs_in[(side * (part // LANES) + pair) * 2 + which]
                grad_probs = dot_back(jnp.where(chosen, mixed, jnp.zeros_like(mixed)), value)
                grad_value = dot_over(probs.astype(LOW), mixed)
                shared = jnp.sum(probs * grad_probs, axis=-1, keepdims=True)
                grad_scores = (probs * (grad_probs - shared)).astype(LOW)
                found.append(
                    (
                        dot_plain(grad_scores, key) * SCALE,
                        dot_over(grad_scores, query) * SCALE,
                        grad_value,
                    )
                )
            for member in range(3):
                pieces[member].append(
                    jnp.where(first_head, found[0][member], found[1][member]).astype(LOW)
                )
        copies[6 + side].wait()
        for member in range(3):
            piece = jnp.concatenate(pieces[member], axis=1)
            store_chunks(
                piece,
                in_buffer,
                in_first[side] + (units + member * part) // LANES,
            )
            if member != 1:
                sums.append(column_sum(piece))
            grad_normed = grad_normed + dot_back(piece, wq[member])
    small_store(small_out, 4 * per, jnp.where(is_first, sums[0], sums[2]))
    small_store(small_out, 4 * per + per // 2, jnp.where(is_first, sums[2], sums[0]))
    small_store(small_out, 5 * per, jnp.where(is_first, sums[1], sums[3]))
    small_store(small_out, 5 * per + per // 2, jnp.where(is_first, sums[3], sums[1]))
    state = with_room(inputs, held)
    unit, inverse = spread_of(state)
    small_store(small_out, 0, column_sum(grad_normed * unit))
    small_store(small_out, 2 * per, column_sum(grad_normed))
    total = grad_middle + norm_back(grad_normed, unit, inverse, gain[index, 0:1])
    grad_out[...] = total[0 : grad_out.shape[0]]
    for copy in extra:
        copy.wait()


class Layout:
    def __init__(self, rows, width, units, joined):
        self.rows = room_for(rows)
        self.width = width
        self.units = units
        self.joined = joined
        part = width // 2
        self.group_chunks = ((units + part) // LANES, (units + 3 * part) // LANES)
        if joined:
            items = (("right", 0), ("right", 1), ("left", 0), ("left", 1))
            self.parcels = ((False, 0, items),)
        else:
            self.parcels = (
                (True, 0, (("right", 0),)),
                (False, 0, (("left", 0),)),
                (False, 1, (("right", 1), ("left", 1))),
            )
        self.bundles = ((0, 1),) if joined else ((0,), (1,))

    def axis_of(self, group):
        return 0 if self.joined else group

    def item_rows(self, item):
        kind, group = item
        return self.width if kind == "left" else 2 * self.group_chunks[group] * self.rows

    def parcel_rows(self, spot):
        return sum(self.item_rows(item) for item in self.parcels[spot][2])

    def place(self, item):
        for spot, (_, _, items) in enumerate(self.parcels):
            if item in items:
                before = items[: items.index(item)]
                return spot, sum(self.item_rows(other) for other in before)

    def segments(self, group):
        fc_chunks = self.units // LANES
        return ((0, 0, fc_chunks), (1, fc_chunks, self.group_chunks[group] - fc_chunks))

    def columns(self, bundle):
        return LANES * sum(self.group_chunks[group] for group in self.bundles[bundle])


def product_kernel(layout, near, *refs):
    parcels = len(layout.parcels)
    bundles = len(layout.bundles)
    rows = layout.rows
    half = layout.width // 2
    own, far, keeps = refs[:parcels], refs[parcels : 2 * parcels], refs[2 * parcels : 2 * parcels + 2]
    refs = refs[2 * parcels + 2 :]
    if near:
        arrived = refs[0]
        keep_outs = refs[1 : 1 + bundles]
        send_outs = refs[1 + bundles : 1 + 2 * bundles]
        refs = refs[1 + 2 * bundles :]
    else:
        outs = refs[0]
        refs = refs[1:]
    here = refs[:2]
    there = refs[2:4]
    lefts, rhs, sems = refs[4:]
    copies = []
    for group in range(2):
        size = layout.group_chunks[group] * rows
        spot, base = layout.place(("right", group))
        if not near:
            base += size
        for source, target in ((own, here), (far, there)):
            copies.append(
                pltpu.make_async_copy(
                    source[spot].at[pl.ds(base, size)], target[group], sems.at[len(copies)]
                )
            )
        spot, base = layout.place(("left", group))
        for member in range(2):
            copies.append(
                pltpu.make_async_copy(
                    keeps[group].at[pl.ds(member * half, half)],
                    lefts.at[2 * group + member, :, pl.ds(0, LANES)],
                    sems.at[len(copies)],
                )
            )
            copies.append(
                pltpu.make_async_copy(
                    far[spot].at[pl.ds(base + member * half, half)],
                    lefts.at[2 * group + member, :, pl.ds(LANES, LANES)],
                    sems.at[len(copies)],
                )
            )
    for copy in copies:
        copy.start()
    rhs[...] = jnp.zeros_like(rhs)
    for copy in copies:
        copy.wait()
    turn = 0
    column = 0
    for bundle, groups in enumerate(layout.bundles):
        local = 0
        for group in groups:
            for member, first, chunks in layout.segments(group):
                for chunk in range(0, chunks, 2):
                    some = min(2, chunks - chunk)
                    slot = turn % rhs.shape[0]
                    turn += 1
                    for step in range(some):
                        lanes = slice(step * LANES, (step + 1) * LANES)
                        at = (first + chunk + step) * rows
                        rhs[slot, 0:rows, lanes] = here[group][at : at + rows, :]
                        rhs[slot, LANES : LANES + rows, lanes] = there[group][at : at + rows, :]
                    product = dot_plain(
                        lefts[2 * group + member], rhs[slot, :, 0 : some * LANES]
                    )
                    cols = slice(column, column + some * LANES)
                    if near:
                        product = product + arrived[:, cols].astype(WIDE)
                        into = slice(local, local + some * LANES)
                        keep_outs[bundle][:, into] = product[0 : half // 2].astype(LOW)
                        send_outs[bundle][:, into] = product[half // 2 : half].astype(LOW)
                    else:
                        outs[:, cols] = product.astype(LOW)
                    column += some * LANES
                    local += some * LANES


IN_VMEM = pl.BlockSpec(memory_space=pltpu.VMEM)
IN_SMEM = pl.BlockSpec(memory_space=pltpu.SMEM)
ANYWHERE = pl.BlockSpec(memory_space=pl.ANY)


def shape_of(dims, kind):
    return jax.ShapeDtypeStruct(dims, kind)


def limits(size):
    return pltpu.CompilerParams(vmem_limit_bytes=size * MIB)


PACE = 50.0


def cost_of(micros):
    return pl.CostEstimate(
        flops=int(micros * PACE * 1.15e9), bytes_accessed=0, transcendentals=0
    )


def after_all(kernel, at, count):
    def call(*refs):
        kernel(*refs[:at], *refs[at + count :])

    return call


def run_forward(state, index, params, places, length, layout, after):
    gain, shift, res_bias, own, far, bias_at = params
    count, width = state.shape
    rows = layout.rows
    part = width // 2
    units = layout.units
    heads = width // HEAD
    weights = [own[0], far[0], own[2], far[2], own[3], far[3], own[4], far[4]]
    biases = [own[1], far[1]]
    causal = length is not None
    args = [places, length if causal else places]
    args += [state, gain, shift, res_bias] + biases + weights
    kernel = functools.partial(forward_kernel, index, causal, bias_at)
    return pl.pallas_call(
        after_all(kernel, len(args), len(after)),
        in_specs=[IN_SMEM] * 2 + [IN_VMEM] * 6 + [ANYWHERE] * (8 + len(after)),
        out_specs=[IN_VMEM] * 8,
        out_shape=[
            shape_of((count, width), WIDE),
            shape_of((2, 3, rows, part), LOW),
            shape_of((heads, rows, rows), WIDE),
            shape_of((rows, width), WIDE),
            shape_of((2, rows, units), WIDE),
            shape_of((2 * layout.group_chunks[0] * rows, LANES), LOW),
            shape_of((width, LANES), LOW),
            shape_of((width, LANES), LOW),
        ],
        scratch_shapes=[pltpu.VMEM(w.shape[1:], LOW) for w in weights]
        + [
            pltpu.VMEM((width, LANES), WIDE),
            pltpu.VMEM((width, LANES), WIDE),
            pltpu.VMEM((rows, width), WIDE),
            pltpu.SemaphoreType.DMA((8,)),
        ],
        compiler_params=limits(64),
        cost_estimate=cost_of(width / 84),
    )(*args, *after)


def run_backward(grad, state, index, params, kept, places, core, layout, after):
    gain, _, _, own, far, _ = params
    heads, probs, middle, hidden, right, send = kept
    late = [spot for spot, parcel in enumerate(layout.parcels) if not parcel[0]]
    count, width = state.shape
    rows = layout.rows
    weights = [own[4], far[4], own[3], far[3], own[2], far[2], own[0], far[0]]
    args = [places, core, grad, state, middle, hidden, heads, probs, gain, right, send]
    args += weights
    kernel = functools.partial(backward_kernel, index, layout)
    return pl.pallas_call(
        after_all(kernel, len(args), len(after)),
        in_specs=[IN_SMEM] * 2 + [IN_VMEM] * 7 + [ANYWHERE] * (10 + len(after)),
        out_specs=[IN_VMEM] * (3 + len(late)),
        out_shape=[
            shape_of((count, width), WIDE),
            shape_of((12 * width // LANES, LANES), WIDE),
            shape_of((width, LANES), LOW),
        ]
        + [shape_of((layout.parcel_rows(spot), LANES), LOW) for spot in late],
        scratch_shapes=[pltpu.VMEM(w.shape[1:], LOW) for w in weights]
        + [
            pltpu.VMEM((width, LANES), WIDE),
            pltpu.VMEM((width, LANES), WIDE),
            pltpu.VMEM((rows, width), WIDE),
            pltpu.SemaphoreType.DMA((8,)),
            pltpu.SemaphoreType.DMA((3,)),
        ],
        compiler_params=limits(64),
        cost_estimate=cost_of(width / 52),
    )(*args, *after)


def run_product(layout, own, far, keeps, arrived, after):
    half = layout.width // 2
    bundles = range(len(layout.bundles))
    columns = [layout.columns(bundle) for bundle in bundles]
    args = list(own) + list(far) + list(keeps)
    in_specs = [ANYWHERE] * len(args)
    near = arrived is not None
    if near:
        args.append(arrived)
        in_specs.append(IN_VMEM)
        out_shape = [shape_of((half // 2, c), LOW) for c in columns] * 2
    else:
        out_shape = [shape_of((half, sum(columns)), LOW)]
    kernel = functools.partial(product_kernel, layout, near)
    return pl.pallas_call(
        after_all(kernel, len(args), len(after)),
        in_specs=in_specs + [ANYWHERE] * len(after),
        out_specs=[IN_VMEM] * len(out_shape),
        out_shape=out_shape,
        scratch_shapes=[
            pltpu.VMEM((chunks * layout.rows, LANES), LOW) for chunks in layout.group_chunks
        ]
        * 2
        + [
            pltpu.VMEM((4, half, 2 * LANES), LOW),
            pltpu.VMEM((4, 2 * LANES, 2 * LANES), LOW),
            pltpu.SemaphoreType.DMA((12,)),
        ],
        compiler_params=limits(64),
        cost_estimate=cost_of(layout.width * (2 if near else 1.4) / 220),
    )(*args, *after)


def join_kernel(count, split, *refs):
    keeps = refs[:count]
    arrived = refs[count : 2 * count]
    outs = refs[2 * count :]
    first = 0
    for keep, come in zip(keeps, arrived):
        cols = slice(first, first + keep.shape[1])
        first += keep.shape[1]
        if split:
            half = keep.shape[0] // 2
            for spot, out in enumerate(outs):
                rows = slice(spot * half, (spot + 1) * half)
                out[:, cols] = (keep[rows].astype(WIDE) + come[rows].astype(WIDE)).astype(LOW)
        else:
            outs[0][:, cols] = (keep[...].astype(WIDE) + come[...].astype(WIDE)).astype(LOW)


def run_join(keeps, arrived, split, after):
    rows = keeps[0].shape[0] // (2 if split else 1)
    columns = sum(keep.shape[1] for keep in keeps)
    kernel = functools.partial(join_kernel, len(keeps), split)
    return pl.pallas_call(
        after_all(kernel, 2 * len(keeps), len(after)),
        in_specs=[IN_VMEM] * (2 * len(keeps)) + [ANYWHERE] * len(after),
        out_specs=[IN_VMEM] * (2 if split else 1),
        out_shape=[shape_of((rows, columns), LOW)] * (2 if split else 1),
        compiler_params=limits(64),
        cost_estimate=cost_of(2.5),
    )(*keeps, *arrived, *after)


def finish_kernel(counts, width, units, *refs):
    part = width // 2
    qkv, out_proj, fc_in, fc_out = refs[sum(counts) :]
    first = 0
    for block, count in enumerate(counts):
        terms = refs[first : first + count]
        first += count

        def total(low, high):
            value = terms[0][:, low:high].astype(WIDE)
            for term in terms[1:]:
                value = value + term[:, low:high].astype(WIDE)
            return value

        fc_out[block] = total(0, units)
        out_proj[block] = total(units, units + part)
        low = units + part
        fc_in[block] = total(low, low + units)
        low += units
        for member in range(3):
            qkv[block, member] = total(low + member * part, low + (member + 1) * part)


def run_finish(blocks, width, units):
    depth = blocks[0][0].shape[0]
    part = width // 2
    count = len(blocks)
    terms = [term for block in blocks for term in block]
    qkv, out_proj, fc_in, fc_out = pl.pallas_call(
        functools.partial(finish_kernel, tuple(len(block) for block in blocks), width, units),
        in_specs=[IN_VMEM] * len(terms),
        out_specs=[IN_VMEM] * 4,
        out_shape=[
            shape_of((count, 3, depth, part), WIDE),
            shape_of((count, depth, part), WIDE),
            shape_of((count, depth, units), WIDE),
            shape_of((count, depth, units), WIDE),
        ],
        compiler_params=limits(64),
        cost_estimate=cost_of(3),
    )(*terms)
    return qkv, out_proj.swapaxes(1, 2), fc_in, fc_out.swapaxes(1, 2)


def small_kernel(widths, own, come, *outs):
    base = 0
    for tower, width in enumerate(widths):
        per = width // LANES
        gains, shifts, qv_bias, fc_in_bias, res_bias = outs[5 * tower : 5 * tower + 5]
        for block in range(gains.shape[0]):
            for target, group in ((gains, 0), (shifts, 2), (qv_bias, 4), (res_bias, 10)):
                for member in range(2):
                    for chunk in range(per):
                        row = base + (group + member) * per + chunk
                        cols = slice(chunk * LANES, (chunk + 1) * LANES)
                        target[block, member : member + 1, cols] = (
                            own[row : row + 1, :] + come[row : row + 1, :]
                        )
            for chunk in range(4 * per):
                row = base + 6 * per + chunk
                fc_in_bias[block : block + 1, chunk * LANES : (chunk + 1) * LANES] = (
                    own[row : row + 1, :] + come[row : row + 1, :]
                )
            base += 12 * per


def run_small(own, come, widths, depth_count):
    out_shape = []
    for width in widths:
        pair = shape_of((depth_count, 2, width), WIDE)
        out_shape += [pair, pair, pair, shape_of((depth_count, 4 * width), WIDE), pair]
    return pl.pallas_call(
        functools.partial(small_kernel, tuple(widths)),
        in_specs=[IN_VMEM] * 2,
        out_specs=[IN_VMEM] * len(out_shape),
        out_shape=out_shape,
        compiler_params=limits(64),
        cost_estimate=cost_of(1.7),
    )(own, come)


def gather_kernel(*refs):
    out = refs[-1]
    first = 0
    for ref in refs[:-1]:
        out[first : first + ref.shape[0], :] = ref[...]
        first += ref.shape[0]


def add_kernel(own, come, out):
    out[...] = own[...] + come[...]


def run_rows(kernel, members, rows, after):
    return pl.pallas_call(
        after_all(kernel, len(members), len(after)),
        in_specs=[IN_VMEM] * len(members) + [ANYWHERE] * len(after),
        out_specs=IN_VMEM,
        out_shape=shape_of((rows, LANES), WIDE),
        compiler_params=limits(64),
        cost_estimate=cost_of(1.5),
    )(*members, *after)


def dp_bits():
    return (lax.axis_size("dp") - 1).bit_length()


def slice_order(order, relative):
    me = lax.axis_index("dp")
    places = jnp.arange(lax.axis_size("dp"), dtype=jnp.int32)
    source = jnp.zeros_like(places)
    for digit, bit in enumerate(order):
        value = (places >> (len(order) - 1 - digit)) & 1
        if digit < relative:
            value = value ^ ((me >> bit) & 1)
        source = source | (value << bit)
    return source


def swap(values, bit):
    size = lax.axis_size("dp")
    return lax.ppermute(values, "dp", [(spot, spot ^ (1 << bit)) for spot in range(size)])


def swap_cores(values):
    return lax.ppermute(values, "tensor", [(0, 1), (1, 0)])


def swap_all(members, name, biases_far, landed):
    found = [
        biases_far if spot == 1 else swap_cores(member) for spot, member in enumerate(members)
    ]
    for spot, member in enumerate(found):
        landed["w" + str(spot) + name] = member
    return found


class Tower:
    def __init__(self, name, landed, inputs, params, cotangent, length, joined, ways, by_sum):
        self.name = name
        self.landed = landed
        self.inputs = inputs
        self.params = params
        self.cotangent = cotangent
        self.length = length
        self.depth_count = params[0].shape[0]
        width = inputs.shape[1]
        self.layout = Layout(inputs.shape[0], width, params[3][3].shape[2], joined)
        self.ways = ways
        self.by_sum = by_sum
        self.states = []
        self.kept = []
        self.grads = {}
        self.smalls = {}
        self.own = {}
        self.far = {}
        self.keeps = {}
        self.crossed = {}
        self.sums = {}

    def send(self, label, index, values, bit):
        come = swap(values, bit)
        self.landed[label + self.name + str(index)] = come
        return come

    def hops(self, index, group):
        way = self.ways[index][group]
        return list(way) + [bit for bit in range(dp_bits()) if bit not in way]

    def order(self, index, group):
        hops = self.hops(index, group)
        if self.by_sum[index]:
            return hops[:2] + sorted(hops[2:], reverse=True), 2
        return hops, dp_bits()

    def post(self, index, spot, parcel):
        label = "p" + str(spot)
        bit = self.hops(index, self.layout.parcels[spot][1])[0]
        self.own[index, spot] = parcel
        self.far[index, spot] = self.send(label, index, parcel, bit)

    def forward(self, index, after):
        state = self.states[-1] if self.states else self.inputs
        places = slice_order(*self.order(index, 1))
        found = run_forward(state, index, self.params, places, self.length, self.layout, after)
        self.states.append(found[0])
        self.kept.append(found[1:])
        if self.layout.parcels[0][0]:
            self.post(index, 0, found[5])
        return found[3]

    def backward(self, index, after):
        grad = self.cotangent if index + 1 == self.depth_count else self.grads[index + 1]
        state = self.inputs if index == 0 else self.states[index - 1]
        heads, probs, middle, hidden, right, keep, send = self.kept[index]
        places = slice_order(*self.order(index, 0))
        core = lax.axis_index("tensor").astype(jnp.int32).reshape(1)
        found = run_backward(
            grad,
            state,
            index,
            self.params,
            (heads, probs, middle, hidden, right, send),
            places,
            core,
            self.layout,
            after,
        )
        self.grads[index] = found[0]
        self.smalls[index] = found[1]
        late = [spot for spot, parcel in enumerate(self.layout.parcels) if not parcel[0]]
        for spot, parcel in zip(late, found[3:]):
            self.post(index, spot, parcel)
        self.keeps[index] = (found[2], keep)
        return found[1]

    def product(self, index, arrived, after):
        spots = range(len(self.layout.parcels))
        return run_product(
            self.layout,
            [self.own[index, spot] for spot in spots],
            [self.far[index, spot] for spot in spots],
            self.keeps[index],
            arrived,
            after,
        )

    def far_product(self, index, after):
        (product,) = self.product(index, None, after)
        self.crossed[index] = swap_cores(product)
        self.landed["t" + self.name + str(index)] = self.crossed[index]
        return product

    def near_product(self, index, after):
        found = self.product(index, self.crossed[index], after)
        bundles = self.layout.bundles
        keep, send = found[: len(bundles)], found[len(bundles) :]
        come = []
        for spot, (groups, part) in enumerate(zip(bundles, send)):
            bit = self.hops(index, groups[0])[1]
            come.append(self.send("h" + str(spot), index, part, bit))
        self.sums[index] = (keep, come, 2)
        return found[0]

    def collect(self, index, after):
        keep, come, hop = self.sums[index]
        if self.by_sum[index]:
            size = lax.axis_size("dp")
            groups = [[spot for spot in range(size) if spot % 4 == low] for low in range(4)]
            (joined,) = run_join(keep, come, False, after)
            found = lax.psum_scatter(
                joined, "dp", scatter_dimension=0, tiled=True, axis_index_groups=groups
            )
            self.sums[index] = ((found,), (), dp_bits())
            return joined
        keep, send = run_join(keep, come, True, after)
        come = self.send("g" + str(hop), index, send, self.hops(index, 0)[hop])
        self.sums[index] = ((keep,), (come,), hop + 1)
        return keep

    def finish(self):
        blocks = []
        for index in range(self.depth_count):
            while self.sums[index][2] < dp_bits():
                self.collect(index, ())
            keep, come, _ = self.sums[index]
            blocks.append(tuple(keep) + tuple(come))
        return run_finish(blocks, self.layout.width, self.layout.units)


class Smalls:
    def __init__(self, landed, towers, axes):
        self.landed = landed
        self.towers = towers
        self.axes = list(axes) + [bit for bit in range(dp_bits()) if bit not in axes]
        self.values = None
        self.come = None
        self.hop = 0

    def step(self, index, after):
        if self.values is None:
            members = [
                tower.smalls[block] for tower in self.towers for block in range(tower.depth_count)
            ]
            rows = sum(member.shape[0] for member in members)
            self.values = run_rows(gather_kernel, members, rows, after)
        else:
            rows = self.values.shape[0]
            self.values = run_rows(add_kernel, [self.values, self.come], rows, after)
        axis = self.axes[self.hop]
        self.come = swap_cores(self.values) if axis is None else swap(self.values, axis)
        self.landed["s" + str(self.hop)] = self.come
        self.hop += 1
        return self.values

    def finish(self):
        while self.hop < len(self.axes):
            self.step(0, ())
        widths = [tower.layout.width for tower in self.towers]
        return run_small(self.values, self.come, widths, self.towers[0].depth_count)


WAYS = {'i': (((1, 0, 2, 3), (0, 1, 2, 3)), ((0, 1, 2, 3), (1, 0, 2, 3))), 'c': (((2, 0, 1, 3), (2, 0, 1, 3)), ((2, 1, 0, 3), (2, 1, 0, 3)))}
PLAN = (
    "Fi0",
    "Fi1+w0c+w2c+w3c",
    "Bi1+w4c",
    "Bi0+p0i0",
    "Fc0+p0i1+p1i1",
    "Fc1",
    "Bc1+p2i1",
    "fi1+p1i0",
    "fi0",
    "Bc0",
    "ni0+ti1",
    "fc1",
    "ni1",
    "nc1",
    "ss0",
    "ji0",
    "fc0",
    "ss0",
    "nc0",
    "ji1",
    "ss0",
    "ji0",
    "ss0",
    "jc1",
    "ss0",
    "jc0",
    "jc1+g3i0",
    "jc0",
)
BY_SUM = (False, True)
SMALL_WAY = (None, 0, 3, 1, 2)


def on_device(
    image_in,
    image_norm_gain,
    image_norm_shift,
    image_qkv,
    image_qv_bias,
    image_out_proj,
    image_fc_in,
    image_fc_in_bias,
    image_fc_out,
    image_res_bias,
    image_cot,
    caption_in,
    caption_norm_gain,
    caption_norm_shift,
    caption_qkv,
    caption_qv_bias,
    caption_out_proj,
    caption_fc_in,
    caption_fc_in_bias,
    caption_fc_out,
    caption_res_bias,
    caption_lengths,
    caption_cot,
):
    landed = {}
    depth_count = image_fc_in_bias.shape[0]
    members = (image_qv_bias, image_fc_in_bias, caption_qv_bias, caption_fc_in_bias)
    biases = jnp.concatenate([member.reshape(depth_count, -1) for member in members], axis=1)
    biases_far = swap_cores(biases)
    caption_bias_at = image_qv_bias[0].size + image_fc_in_bias[0].size
    image_own = (image_qkv, biases, image_out_proj, image_fc_in, image_fc_out)
    caption_own = (caption_qkv, biases, caption_out_proj, caption_fc_in, caption_fc_out)
    image_far = swap_all(image_own, "i", biases_far, landed)
    caption_far = swap_all(caption_own, "c", biases_far, landed)
    image_params = (
        image_norm_gain,
        image_norm_shift,
        image_res_bias,
        image_own,
        image_far,
        0,
    )
    caption_params = (
        caption_norm_gain,
        caption_norm_shift,
        caption_res_bias,
        caption_own,
        caption_far,
        caption_bias_at,
    )
    length = lax.dynamic_slice_in_dim(caption_lengths, lax.axis_index("tensor"), 1)
    caption = Tower(
        "c", landed, caption_in, caption_params, caption_cot, length, True, WAYS["c"], (False, False)
    )
    image = Tower(
        "i", landed, image_in, image_params, image_cot, None, False, WAYS["i"], BY_SUM
    )
    smalls = Smalls(landed, (image, caption), SMALL_WAY)
    kinds = {
        "F": ("forward", 0),
        "B": ("backward", 0),
        "f": ("far_product", 0),
        "n": ("near_product", 0),
        "j": ("collect", 0),
        "s": ("step", 0),
    }
    towers = {"i": image, "c": caption, "s": smalls}
    after = caption_norm_gain
    for step in PLAN:
        name, *waits = step.split("+")
        member = towers[name[1]]
        before = [after] + [landed[wait] for wait in waits]
        after = getattr(member, kinds[name[0]][0])(int(name[2]), before)
    caption_matrix = caption.finish()
    image_matrix = image.finish()
    small = smalls.finish()
    outs = []
    for tower, few, matrix in ((image, small[:5], image_matrix), (caption, small[5:], caption_matrix)):
        outs += [
            tower.states[-1],
            tower.grads[0],
            few[0],
            few[1],
            matrix[0],
            few[2],
            matrix[1],
            matrix[2],
            few[3],
            matrix[3],
            few[4],
        ]
    return tuple(outs)


def solution(mesh):
    placed = (
        P(("dp", "tensor"), None),
        P(),
        P(),
        P(None, None, None, "tensor"),
        P(None, None, "tensor"),
        P(None, "tensor", None),
        P(None, None, "tensor"),
        P(None, "tensor"),
        P(None, "tensor", None),
        P(),
        P(("dp", "tensor"), None),
        P(("dp", "tensor"), None),
        P(),
        P(),
        P(None, None, None, "tensor"),
        P(None, None, "tensor"),
        P(None, "tensor", None),
        P(None, None, "tensor"),
        P(None, "tensor"),
        P(None, "tensor", None),
        P(),
        P("dp"),
        P(("dp", "tensor"), None),
    )
    return jax.shard_map(
        on_device,
        mesh=mesh,
        in_specs=placed,
        out_specs=(
            P(("dp", "tensor"), None),
            P(("dp", "tensor"), None),
            P(),
            P(),
            P(None, None, "dp", "tensor"),
            P(),
            P(None, "tensor", "dp"),
            P(None, "dp", "tensor"),
            P(),
            P(None, "tensor", "dp"),
            P(),
            P(("dp", "tensor"), None),
            P(("dp", "tensor"), None),
            P(),
            P(),
            P(None, None, "dp", "tensor"),
            P(),
            P(None, "tensor", "dp"),
            P(None, "dp", "tensor"),
            P(),
            P(None, "tensor", "dp"),
            P(),
        ),
        check_vma=False,
    )
```

```python
import functools

import jax
import jax.numpy as jnp
from jax import lax
from jax.experimental import pallas as pl
from jax.experimental.pallas import tpu as pltpu
from jax.sharding import PartitionSpec as P

HEAD = 64
PATCHES = 50
CTX = 77
EPS = 1e-05
SCALE = HEAD ** (-0.5)
LOW = jnp.bfloat16
WIDE = jnp.float32
MIB = 1024 * 1024
LANES = 128


def dot_plain(first, second):
    return jnp.dot(first, second, preferred_element_type=WIDE)


def dot_back(first, second):
    return lax.dot_general(first, second, (((1,), (1,)), ((), ())), preferred_element_type=WIDE)


def dot_over(first, second):
    return lax.dot_general(first, second, (((0,), (0,)), ((), ())), preferred_element_type=WIDE)


def room_for(rows):
    return -(-rows // 16) * 16


def spread_of(values):
    centred = values - jnp.mean(values, axis=-1, keepdims=True)
    inverse = lax.rsqrt(jnp.mean(centred * centred, axis=-1, keepdims=True) + EPS)
    return centred * inverse, inverse


def norm_back(grad, unit, inverse, gain):
    scaled = grad * gain
    return inverse * (
        scaled
        - jnp.mean(scaled, axis=-1, keepdims=True)
        - unit * jnp.mean(scaled * unit, axis=-1, keepdims=True)
    )


def column_sum(values):
    return jnp.sum(values.astype(WIDE), axis=0, keepdims=True)


def allowed_keys(rows, length):
    query = lax.broadcasted_iota(jnp.int32, (rows, rows), 0)
    key = lax.broadcasted_iota(jnp.int32, (rows, rows), 1)
    if length is None:
        return (query // PATCHES) == (key // PATCHES)
    return (key <= query) & (key < length)


def store_left(values, member, places, first_place, turned, sorted_rows, keep, send, send_base):
    rows, width = values.shape
    wide = values.astype(WIDE)
    if rows < LANES:
        wide = jnp.concatenate([wide, jnp.zeros((LANES - rows, width), WIDE)], axis=0)
    turned[...] = wide.T
    count = places.shape[1]
    depth = width // count
    half = width // 2
    if depth % 16:

        def move(row, carry):
            source = places[first_place, row // depth] * depth + row % depth
            sorted_rows[pl.ds(row, 1), :] = turned[pl.ds(source, 1), :]
            return carry

        lax.fori_loop(0, width, move, 0)
        keep[member * half : (member + 1) * half, :] = sorted_rows[0:half, :].astype(LOW)
        send[send_base : send_base + half, :] = sorted_rows[half:width, :].astype(LOW)
        return
    for spot in range(count):
        first = pl.multiple_of(places[first_place, spot] * depth, depth)
        block = turned[pl.ds(first, depth), :].astype(LOW)
        if spot < count // 2:
            first = member * half + spot * depth
            keep[first : first + depth, :] = block
        else:
            first = send_base + spot * depth - half
            send[first : first + depth, :] = block


def store_chunks(values, target, first_chunk):
    rows = values.shape[0]
    for chunk in range(values.shape[1] // LANES):
        first = (first_chunk + chunk) * rows
        target[first : first + rows, :] = values[:, chunk * LANES : (chunk + 1) * LANES]


class Mover:
    def __init__(self, sems):
        self.sems = sems
        self.used = 0
        self.leaving = []

    def pull(self, source, target):
        copy = pltpu.make_async_copy(source, target, self.sems.at[self.used])
        self.used += 1
        copy.start()
        return copy

    def push(self, source, target):
        self.leaving.append(self.pull(source, target))

    def finish(self):
        for copy in self.leaving:
            copy.wait()


class Loader:
    def __init__(self, mover, pairs, ahead):
        self.mover = mover
        self.pairs = pairs
        self.ahead = ahead
        self.copies = []
        self.landed = set()

    def start(self, upto):
        while len(self.copies) < min(upto, len(self.pairs)):
            self.copies.append(self.mover.pull(*self.pairs[len(self.copies)]))

    def need(self, spot):
        self.start(spot + 1 + self.ahead)
        if spot not in self.landed:
            self.landed.add(spot)
            self.copies[spot].wait()


def forward_block(block, causal, bias_at, length, loader, mover, data, layout):
    rows, width = layout.rows, layout.width
    part = width // 2
    units = layout.units
    heads_of = part // LANES
    gain, shift, res_bias = data["gain"], data["shift"], data["res_bias"]
    biases = (data["bias_own"], data["bias_far"])
    heads, probs_out = data["heads"], data["probs"]
    first_weight = 8 * block
    state = data["states"][block]
    unit, _ = spread_of(state)
    normed = (unit * gain[block, 0:1] + shift[block, 0:1]).astype(LOW)
    mask = allowed_keys(rows, length[0] if causal else None)
    lane = lax.broadcasted_iota(jnp.int32, (rows, LANES), 1)
    first_head = lane < HEAD
    row = slice(block, block + 1)
    for side in range(2):
        loader.need(first_weight + side)
        wq = data["wq"][side]
        bias = biases[side]
        first = bias[row, bias_at : bias_at + part]
        second = bias[row, bias_at + part : bias_at + width]
        heads[block, side, 0] = (dot_plain(normed, wq[block, 0]) + first).astype(LOW)
        heads[block, side, 1] = dot_plain(normed, wq[block, 1]).astype(LOW)
        heads[block, side, 2] = (dot_plain(normed, wq[block, 2]) + second).astype(LOW)
    data["left"](normed, block, QKV)
    middle = state + res_bias[block, 0:1]
    for side in range(2):
        pieces = []
        for pair in range(heads_of):
            cols = slice(pair * LANES, (pair + 1) * LANES)
            query = heads[block, side, 0, :, cols]
            key = heads[block, side, 1, :, cols]
            value = heads[block, side, 2, :, cols]
            mixed = []
            for which in range(2):
                chosen = first_head if which == 0 else ~first_head
                scores = dot_back(jnp.where(chosen, query, jnp.zeros_like(query)), key) * SCALE
                scores = jnp.where(mask, scores, -1000000000.0)
                weights = jnp.exp(scores - jnp.max(scores, axis=-1, keepdims=True))
                probs = weights / jnp.sum(weights, axis=-1, keepdims=True)
                probs_out[block, (side * heads_of + pair) * 2 + which] = probs
                mixed.append(dot_plain(probs.astype(LOW), value))
            pieces.append(jnp.where(first_head, mixed[0], mixed[1]).astype(LOW))
        mixed_rows = jnp.concatenate(pieces, axis=1)
        data["right"](mixed_rows, block, OUT_PROJ, side, 0)
        loader.need(first_weight + 2 + side)
        middle = middle + dot_plain(mixed_rows, data["wo"][side][block])
    data["middle"][block] = middle
    unit, _ = spread_of(middle)
    normed_two = (unit * gain[block, 1:2] + shift[block, 1:2]).astype(LOW)
    data["left"](normed_two, block, FC_IN)
    total = middle + res_bias[block, 1:2]
    for side in range(2):
        loader.need(first_weight + 4 + 2 * side)
        first = bias_at + width
        hidden = dot_plain(normed_two, data["wi"][side][block])
        hidden = hidden + biases[side][row, first : first + units]
        data["hidden"][block, side] = hidden
        active = (hidden * jax.nn.sigmoid(1.702 * hidden)).astype(LOW)
        data["right"](active, block, FC_OUT, side, 0)
        loader.need(first_weight + 5 + 2 * side)
        total = total + dot_plain(active, data["wf"][side][block])
    return total


def small_store(small, group, values):
    count = values.shape[1] // LANES
    for chunk in range(count):
        row = group + chunk
        small[row : row + 1, :] = values[:, chunk * LANES : (chunk + 1) * LANES]


def backward_block(block, grad, is_first, mover, data, layout):
    rows, width = layout.rows, layout.width
    part = width // 2
    units = layout.units
    heads_of = part // LANES
    gain, heads, probs_in = data["gain"], data["heads"], data["probs"]
    per = width // LANES
    small = data["small"]
    low = 12 * per * block
    small_store(small, low + 11 * per, column_sum(grad))
    branch_two = grad.astype(LOW)
    grad_normed = jnp.zeros((rows, width), WIDE)
    sums = []
    for side in range(2):
        grad_active = dot_back(branch_two, data["wf"][side][block])
        hidden = data["hidden"][block, side]
        sigma = jax.nn.sigmoid(1.702 * hidden)
        grad_hidden = (
            grad_active * (sigma + 1.702 * hidden * sigma * (1.0 - sigma))
        ).astype(LOW)
        data["right"](grad_hidden, block, FC_IN, side, 0)
        sums.append(column_sum(grad_hidden))
        grad_normed = grad_normed + dot_back(grad_hidden, data["wi"][side][block])
    data["left"](branch_two, block, FC_OUT)
    small_store(small, low + 6 * per, jnp.where(is_first, sums[0], sums[1]))
    small_store(small, low + 8 * per, jnp.where(is_first, sums[1], sums[0]))
    unit, inverse = spread_of(data["middle"][block])
    small_store(small, low + per, column_sum(grad_normed * unit))
    small_store(small, low + 3 * per, column_sum(grad_normed))
    grad_middle = grad + norm_back(grad_normed, unit, inverse, gain[block, 1:2])
    small_store(small, low + 10 * per, column_sum(grad_middle))
    branch_one = grad_middle.astype(LOW)
    data["left"](branch_one, block, OUT_PROJ)
    lane = lax.broadcasted_iota(jnp.int32, (rows, LANES), 1)
    first_head = lane < HEAD
    grad_normed = jnp.zeros((rows, width), WIDE)
    sums = []
    for side in range(2):
        grad_mixed = dot_back(branch_one, data["wo"][side][block]).astype(LOW)
        pieces = [[], [], []]
        for pair in range(heads_of):
            cols = slice(pair * LANES, (pair + 1) * LANES)
            query = heads[block, side, 0, :, cols]
            key = heads[block, side, 1, :, cols]
            value = heads[block, side, 2, :, cols]
            mixed = grad_mixed[:, cols]
            found = []
            for which in range(2):
                chosen = first_head if which == 0 else ~first_head
                probs = probs_in[block, (side * heads_of + pair) * 2 + which]
                grad_probs = dot_back(jnp.where(chosen, mixed, jnp.zeros_like(mixed)), value)
                grad_value = dot_over(probs.astype(LOW), mixed)
                shared = jnp.sum(probs * grad_probs, axis=-1, keepdims=True)
                grad_scores = (probs * (grad_probs - shared)).astype(LOW)
                found.append(
                    (
                        dot_plain(grad_scores, key) * SCALE,
                        dot_over(grad_scores, query) * SCALE,
                        grad_value,
                    )
                )
            for member in range(3):
                pieces[member].append(
                    jnp.where(first_head, found[0][member], found[1][member]).astype(LOW)
                )
        joined = [jnp.concatenate(piece, axis=1) for piece in pieces]
        for member, piece in enumerate(joined):
            data["right"](piece, block, QKV, side, member * part // LANES)
            if member != 1:
                sums.append(column_sum(piece))
            grad_normed = grad_normed + dot_back(piece, data["wq"][side][block, member])
    small_store(small, low + 4 * per, jnp.where(is_first, sums[0], sums[2]))
    small_store(small, low + 4 * per + per // 2, jnp.where(is_first, sums[2], sums[0]))
    small_store(small, low + 5 * per, jnp.where(is_first, sums[1], sums[3]))
    small_store(small, low + 5 * per + per // 2, jnp.where(is_first, sums[3], sums[1]))
    unit, inverse = spread_of(data["states"][block])
    small_store(small, low, column_sum(grad_normed * unit))
    small_store(small, low + 2 * per, column_sum(grad_normed))
    return grad_middle + norm_back(grad_normed, unit, inverse, gain[block, 0:1])


def tower_kernel(layout, count, causal, bias_at, places, core, length, *refs):
    spots = range(len(layout.streams))
    ins, refs = refs[:15], refs[15:]
    fixed = 3 + count
    out_count = fixed + count * len(layout.streams)
    outs, refs = refs[:out_count], refs[out_count:]
    holds, refs = refs[:15], refs[15:]
    results, refs = refs[:out_count], refs[out_count:]
    heads, probs, middle, states, hidden, turned, sorted_rows, sems = refs
    mover = Mover(sems)
    first_in = [mover.pull(source, target) for source, target in zip(ins[:7], holds[:7])]
    inputs, cotangent, gain, shift, res_bias, bias_own, bias_far = holds[:7]
    pairs = [
        (ins[7 + spot].at[block], holds[7 + spot].at[block])
        for block in range(count)
        for spot in (0, 1, 2, 3, 4, 6, 5, 7)
    ]
    loader = Loader(mover, pairs, 5)
    loader.start(4)
    wq0, wq1, wo0, wo1, wi0, wi1, wf0, wf1 = holds[7:]
    output, grad_out, small = results[:3]
    keeps, keep_outs = results[3:fixed], outs[3:fixed]
    parcels = [
        [results[fixed + block * len(spots) + spot] for spot in spots] for block in range(count)
    ]
    parcel_outs = [
        [outs[fixed + block * len(spots) + spot] for spot in spots] for block in range(count)
    ]
    half = layout.width // 2

    def ship(block, spot, base, size):
        piece = pl.ds(base, size)
        mover.push(parcels[block][spot].at[piece], parcel_outs[block][spot].at[piece])

    def left(values, block, matrix):
        spot, base = layout.left_place(matrix)
        store_left(
            values,
            matrix,
            places,
            block * len(spots) + spot,
            turned,
            sorted_rows,
            keeps[block],
            parcels[block][spot],
            base,
        )
        ship(block, spot, base, half)
        kept = pl.ds(matrix * half, half)
        mover.push(keeps[block].at[kept], keep_outs[block].at[kept])

    def right(values, block, matrix, side, chunk):
        spot, base = layout.right_place(matrix, side)
        store_chunks(values, parcels[block][spot], base // layout.rows + chunk)
        size = layout.chunks[matrix] * layout.rows
        if (chunk * LANES + values.shape[1]) == layout.chunks[matrix] * LANES:
            ship(block, spot, base, size)

    data = {
        "gain": gain, "shift": shift, "res_bias": res_bias, "bias_own": bias_own,
        "bias_far": bias_far, "heads": heads, "probs": probs, "middle": middle,
        "states": states, "hidden": hidden, "small": small,
        "wq": (wq0, wq1), "wo": (wo0, wo1), "wi": (wi0, wi1), "wf": (wf0, wf1),
        "left": left, "right": right,
    }
    for copy in first_in:
        copy.wait()
    states[0] = jnp.zeros(states.shape[1:], WIDE)
    states[0, 0 : inputs.shape[0]] = inputs[...].astype(WIDE)
    for block in range(count):
        total = forward_block(block, causal, bias_at, length, loader, mover, data, layout)
        if block + 1 < count:
            states[block + 1] = total
    output[...] = total[0 : output.shape[0]]
    mover.push(output, outs[0])
    states[count] = jnp.zeros(states.shape[1:], WIDE)
    states[count, 0 : inputs.shape[0]] = cotangent[...]
    grad = states[count]
    is_first = core[0] == 0
    for block in reversed(range(count)):
        grad = backward_block(block, grad, is_first, mover, data, layout)
    grad_out[...] = grad[0 : grad_out.shape[0]]
    mover.push(grad_out, outs[1])
    mover.push(small, outs[2])
    mover.finish()


FC_OUT, OUT_PROJ, FC_IN, QKV = range(4)


class Layout:
    def __init__(self, rows, width, units, streams):
        self.rows = room_for(rows)
        self.width = width
        self.units = units
        self.streams = streams
        part = width // 2
        self.chunks = (units // LANES, part // LANES, units // LANES, 3 * part // LANES)

    def stream_of(self, matrix):
        for spot, matrices in enumerate(self.streams):
            if matrix in matrices:
                return spot, matrices[: matrices.index(matrix)]

    def right_place(self, matrix, side):
        spot, before = self.stream_of(matrix)
        chunks = sum(2 * self.chunks[other] for other in before) + side * self.chunks[matrix]
        return spot, chunks * self.rows

    def left_place(self, matrix):
        spot, before = self.stream_of(matrix)
        chunks = sum(2 * self.chunks[other] for other in self.streams[spot])
        return spot, chunks * self.rows + len(before) * self.width // 2

    def parcel_rows(self, spot):
        chunks = sum(2 * self.chunks[other] for other in self.streams[spot])
        return chunks * self.rows + len(self.streams[spot]) * self.width // 2

    def columns(self, spot):
        return LANES * sum(self.chunks[matrix] for matrix in self.streams[spot])


def product_kernel(layout, near, *refs):
    streams = layout.streams
    rows = layout.rows
    half = layout.width // 2
    own, far, keep = refs[: len(streams)], refs[len(streams) : 2 * len(streams)], refs[2 * len(streams)]
    refs = refs[2 * len(streams) + 1 :]
    count = 2 * len(streams) if near else 1
    if near:
        arrived_in, refs = refs[0], refs[1:]
    outs, results, refs = refs[:count], refs[count : 2 * count], refs[2 * count :]
    if near:
        arrived, refs = refs[0], refs[1:]
    here, there = refs[:4], refs[4:8]
    lefts, rhs, sems = refs[8:]
    mover = Mover(sems)
    waits = {}
    column = 0
    for matrices in streams:
        for matrix in matrices:
            spot, base = layout.right_place(matrix, 0 if near else 1)
            piece = pl.ds(base, layout.chunks[matrix] * rows)
            left_base = layout.left_place(matrix)[1]
            found = [
                mover.pull(
                    keep.at[pl.ds(matrix * half, half)], lefts.at[matrix, :, pl.ds(0, LANES)]
                ),
                mover.pull(
                    far[spot].at[pl.ds(left_base, half)],
                    lefts.at[matrix, :, pl.ds(LANES, LANES)],
                ),
                mover.pull(own[spot].at[piece], here[matrix]),
                mover.pull(far[spot].at[piece], there[matrix]),
            ]
            size = layout.chunks[matrix] * LANES
            if near:
                cols = pl.ds(column, size)
                found.append(mover.pull(arrived_in.at[:, cols], arrived.at[:, cols]))
            column += size
            waits[matrix] = found
    rhs[...] = jnp.zeros_like(rhs)
    turn = 0
    column = 0
    for spot, matrices in enumerate(streams):
        local = 0
        for matrix in matrices:
            for copy in waits[matrix]:
                copy.wait()
            begun = (column, local)
            for chunk in range(0, layout.chunks[matrix], 2):
                some = min(2, layout.chunks[matrix] - chunk)
                slot = turn % rhs.shape[0]
                turn += 1
                for step in range(some):
                    lanes = slice(step * LANES, (step + 1) * LANES)
                    at = (chunk + step) * rows
                    rhs[slot, 0:rows, lanes] = here[matrix][at : at + rows, :]
                    rhs[slot, LANES : LANES + rows, lanes] = there[matrix][at : at + rows, :]
                product = dot_plain(lefts[matrix], rhs[slot, :, 0 : some * LANES])
                cols = slice(column, column + some * LANES)
                if near:
                    product = product + arrived[:, cols].astype(WIDE)
                    into = slice(local, local + some * LANES)
                    results[spot][:, into] = product[0 : half // 2].astype(LOW)
                    results[len(streams) + spot][:, into] = product[half // 2 : half].astype(LOW)
                else:
                    results[0][:, cols] = product.astype(LOW)
                column += some * LANES
                local += some * LANES
            if near:
                cols = pl.ds(begun[1], local - begun[1])
                for out in (spot, len(streams) + spot):
                    mover.push(results[out].at[:, cols], outs[out].at[:, cols])
            else:
                cols = pl.ds(begun[0], column - begun[0])
                mover.push(results[0].at[:, cols], outs[0].at[:, cols])
    mover.finish()


IN_VMEM = pl.BlockSpec(memory_space=pltpu.VMEM)
IN_SMEM = pl.BlockSpec(memory_space=pltpu.SMEM)
ANYWHERE = pl.BlockSpec(memory_space=pl.ANY)


def shape_of(dims, kind):
    return jax.ShapeDtypeStruct(dims, kind)


def limits(size):
    return pltpu.CompilerParams(vmem_limit_bytes=size * MIB)


def cost_of(micros):
    return pl.CostEstimate(flops=int(micros * 6e10), bytes_accessed=0, transcendentals=0)


def after_all(kernel, at, count):
    def call(*refs):
        kernel(*refs[:at], *refs[at + count :])

    return call


def run_tower(inputs, cotangent, params, places, core, length, layout, after):
    gain, shift, res_bias, own, far, bias_at = params
    entries, width = inputs.shape
    count = gain.shape[0]
    rows = layout.rows
    part = width // 2
    units = layout.units
    weights = [own[0], far[0], own[2], far[2], own[3], far[3], own[4], far[4]]
    causal = length is not None
    scalars = [places, core, length if causal else core]
    arrays = [inputs, cotangent, gain, shift, res_bias, own[1], far[1]] + weights
    outs = [
        ((entries, width), WIDE),
        ((entries, width), WIDE),
        ((count * 12 * width // LANES, LANES), WIDE),
    ]
    outs += [((2 * width, LANES), LOW)] * count
    outs += [((layout.parcel_rows(spot), LANES), LOW) for spot in range(len(layout.streams))] * count
    holds = [(member.shape, member.dtype) for member in arrays]
    work = [
        ((count, 2, 3, rows, part), LOW),
        ((count, width // HEAD, rows, rows), WIDE),
        ((count, rows, width), WIDE),
        ((count + 1, rows, width), WIDE),
        ((count, 2, rows, units), WIDE),
        ((width, LANES), WIDE),
        ((width, LANES), WIDE),
    ]
    kernel = functools.partial(tower_kernel, layout, count, causal, bias_at)
    return pl.pallas_call(
        after_all(kernel, 18, len(after)),
        in_specs=[IN_SMEM] * 3 + [ANYWHERE] * (15 + len(after)),
        out_specs=[ANYWHERE] * len(outs),
        out_shape=[shape_of(*out) for out in outs],
        scratch_shapes=[pltpu.VMEM(*hold) for hold in holds + outs + work]
        + [pltpu.SemaphoreType.DMA((96,))],
        compiler_params=limits(64),
        cost_estimate=cost_of(width / 20),
    )(*scalars, *arrays, *after)


def run_product(layout, own, far, keep, arrived, after):
    half = layout.width // 2
    columns = [layout.columns(spot) for spot in range(len(layout.streams))]
    args = list(own) + list(far) + [keep]
    near = arrived is not None
    scratch = []
    if near:
        args.append(arrived)
        outs = [((half // 2, c), LOW) for c in columns] * 2
        scratch = [(arrived.shape, LOW)]
    else:
        outs = [((half, sum(columns)), LOW)]
    pieces = [((chunks * layout.rows, LANES), LOW) for chunks in layout.chunks] * 2
    kernel = functools.partial(product_kernel, layout, near)
    return pl.pallas_call(
        after_all(kernel, len(args), len(after)),
        in_specs=[ANYWHERE] * (len(args) + len(after)),
        out_specs=[ANYWHERE] * len(outs),
        out_shape=[shape_of(*out) for out in outs],
        scratch_shapes=[pltpu.VMEM(*hold) for hold in outs + scratch + pieces]
        + [
            pltpu.VMEM((4, half, 2 * LANES), LOW),
            pltpu.VMEM((4, 2 * LANES, 2 * LANES), LOW),
            pltpu.SemaphoreType.DMA((32,)),
        ],
        compiler_params=limits(64),
        cost_estimate=cost_of(layout.width * (2 if near else 1.4) / 220),
    )(*args, *after)


def join_kernel(keep_in, come_in, keep, send):
    half = keep.shape[0]
    for spot, out in enumerate((keep, send)):
        rows = slice(spot * half, (spot + 1) * half)
        out[...] = (keep_in[rows].astype(WIDE) + come_in[rows].astype(WIDE)).astype(LOW)


def run_join(keep, come, after):
    half = shape_of((keep.shape[0] // 2, keep.shape[1]), LOW)
    return pl.pallas_call(
        after_all(join_kernel, 2, len(after)),
        in_specs=[IN_VMEM] * 2 + [ANYWHERE] * len(after),
        out_specs=[IN_VMEM] * 2,
        out_shape=[half, half],
        compiler_params=limits(64),
        cost_estimate=cost_of(2.5),
    )(keep, come, *after)


def finish_kernel(streams, widths, count, *refs):
    outs = refs[2 * len(streams) * count :]
    for block in range(count):
        for spot, matrices in enumerate(streams):
            at = 2 * (block * len(streams) + spot)
            keep, come = refs[at], refs[at + 1]
            first = 0
            for matrix in matrices:
                cols = slice(first, first + widths[matrix])
                first += widths[matrix]
                total = keep[:, cols].astype(WIDE) + come[:, cols].astype(WIDE)
                if matrix == QKV:
                    part = widths[matrix] // 3
                    for member in range(3):
                        outs[matrix][block, member] = total[:, member * part : (member + 1) * part]
                else:
                    outs[matrix][block] = total


def run_finish(blocks, layout, after):
    terms = [term for block in blocks for pair in block for term in pair]
    count = len(blocks)
    depth = terms[0].shape[0]
    widths = [chunks * LANES for chunks in layout.chunks]
    dims = [(count, depth, width) for width in widths]
    dims[QKV] = (count, 3, depth, widths[QKV] // 3)
    kernel = functools.partial(finish_kernel, layout.streams, widths, count)
    fc_out, out_proj, fc_in, qkv = pl.pallas_call(
        after_all(kernel, len(terms), len(after)),
        in_specs=[IN_VMEM] * len(terms) + [ANYWHERE] * len(after),
        out_specs=[IN_VMEM] * 4,
        out_shape=[shape_of(dim, WIDE) for dim in dims],
        compiler_params=limits(64),
        cost_estimate=cost_of(3),
    )(*terms, *after)
    return qkv, out_proj.swapaxes(1, 2), fc_in, fc_out.swapaxes(1, 2)


def small_kernel(widths, own, come, *outs):
    base = 0
    for tower, width in enumerate(widths):
        per = width // LANES
        gains, shifts, qv_bias, fc_in_bias, res_bias = outs[5 * tower : 5 * tower + 5]
        for block in range(gains.shape[0]):
            for target, group in ((gains, 0), (shifts, 2), (qv_bias, 4), (res_bias, 10)):
                for member in range(2):
                    for chunk in range(per):
                        row = base + (group + member) * per + chunk
                        cols = slice(chunk * LANES, (chunk + 1) * LANES)
                        target[block, member : member + 1, cols] = (
                            own[row : row + 1, :] + come[row : row + 1, :]
                        )
            for chunk in range(4 * per):
                row = base + 6 * per + chunk
                fc_in_bias[block : block + 1, chunk * LANES : (chunk + 1) * LANES] = (
                    own[row : row + 1, :] + come[row : row + 1, :]
                )
            base += 12 * per


def run_small(own, come, widths, depth_count, after):
    out_shape = []
    for width in widths:
        pair = shape_of((depth_count, 2, width), WIDE)
        out_shape += [pair, pair, pair, shape_of((depth_count, 4 * width), WIDE), pair]
    return pl.pallas_call(
        after_all(functools.partial(small_kernel, tuple(widths)), 2, len(after)),
        in_specs=[IN_VMEM] * 2 + [ANYWHERE] * len(after),
        out_specs=[IN_VMEM] * len(out_shape),
        out_shape=out_shape,
        compiler_params=limits(64),
        cost_estimate=cost_of(1.7),
    )(own, come, *after)


def gather_kernel(*refs):
    out = refs[-1]
    first = 0
    for ref in refs[:-1]:
        out[first : first + ref.shape[0], :] = ref[...]
        first += ref.shape[0]


def add_kernel(own, come, out):
    out[...] = own[...] + come[...]


def run_rows(kernel, members, rows, after):
    return pl.pallas_call(
        after_all(kernel, len(members), len(after)),
        in_specs=[IN_VMEM] * len(members) + [ANYWHERE] * len(after),
        out_specs=IN_VMEM,
        out_shape=shape_of((rows, LANES), WIDE),
        compiler_params=limits(64),
        cost_estimate=cost_of(1.5),
    )(*members, *after)


def dp_bits():
    return (lax.axis_size("dp") - 1).bit_length()


def slice_order(order):
    places = jnp.arange(lax.axis_size("dp"), dtype=jnp.int32)
    source = jnp.zeros_like(places)
    for digit, bit in enumerate(order):
        source = source | (((places >> (len(order) - 1 - digit)) & 1) << bit)
    return source ^ lax.axis_index("dp").astype(jnp.int32)


def swap(values, bit):
    size = lax.axis_size("dp")
    return lax.ppermute(values, "dp", [(spot, spot ^ (1 << bit)) for spot in range(size)])


def swap_cores(values):
    return lax.ppermute(values, "tensor", [(0, 1), (1, 0)])


def swap_all(members, name, biases_far, landed):
    found = [
        biases_far if spot == 1 else swap_cores(member) for spot, member in enumerate(members)
    ]
    for spot, member in enumerate(found):
        landed["w" + str(spot) + name] = member
    return found


class Tower:
    def __init__(self, name, landed, inputs, params, cotangent, length, streams, ways):
        self.name = name
        self.landed = landed
        self.inputs = inputs
        self.params = params
        self.cotangent = cotangent
        self.length = length
        self.depth_count = params[0].shape[0]
        self.layout = Layout(inputs.shape[0], inputs.shape[1], params[3][3].shape[2], streams)
        self.ways = ways
        self.own = {}
        self.far = {}
        self.keep = {}
        self.crossed = {}
        self.sums = {}

    def send(self, label, values, bit):
        self.landed[label] = come = swap(values, bit)
        return come

    def hops(self, index, stream):
        way = self.ways[index][stream]
        return list(way) + [bit for bit in range(dp_bits()) if bit not in way]

    def whole(self, _, stream, after):
        spots = range(len(self.layout.streams))
        blocks = range(self.depth_count)
        places = jnp.stack(
            [slice_order(self.hops(index, spot)) for index in blocks for spot in spots]
        )
        core = lax.axis_index("tensor").astype(jnp.int32).reshape(1)
        found = run_tower(
            self.inputs,
            self.cotangent,
            self.params,
            places,
            core,
            self.length,
            self.layout,
            after,
        )
        self.output, self.grad, self.small = found[:3]
        first = 3 + len(blocks)
        for index in reversed(blocks):
            self.keep[index] = found[3 + index]
            for spot in spots:
                parcel = found[first + index * len(spots) + spot]
                self.own[index, spot] = parcel
                label = "p%s%d%d" % (self.name, index, spot)
                self.far[index, spot] = self.send(label, parcel, self.hops(index, spot)[0])
        return self.small

    def product(self, index, arrived, after):
        spots = range(len(self.layout.streams))
        return run_product(
            self.layout,
            [self.own[index, spot] for spot in spots],
            [self.far[index, spot] for spot in spots],
            self.keep[index],
            arrived,
            after,
        )

    def far_product(self, index, stream, after):
        (product,) = self.product(index, None, after)
        self.crossed[index] = swap_cores(product)
        self.landed["t%s%d0" % (self.name, index)] = self.crossed[index]
        return product

    def near_product(self, index, stream, after):
        found = self.product(index, self.crossed[index], after)
        spots = range(len(self.layout.streams))
        for spot in spots:
            keep, send = found[spot], found[len(spots) + spot]
            label = "h%s%d%d" % (self.name, index, spot)
            come = self.send(label, send, self.hops(index, spot)[1])
            self.sums[index, spot] = (keep, come, 2)
        return found[0]

    def collect(self, index, stream, after):
        keep, come, hop = self.sums[index, stream]
        keep, send = run_join(keep, come, after)
        label = "g%s%d%d%d" % (self.name, index, stream, hop)
        come = self.send(label, send, self.hops(index, stream)[hop])
        self.sums[index, stream] = (keep, come, hop + 1)
        return keep

    def finish(self, _, stream, after):
        spots = range(len(self.layout.streams))
        blocks = []
        for index in range(self.depth_count):
            for spot in spots:
                while self.sums[index, spot][2] < dp_bits():
                    self.collect(index, spot, ())
            blocks.append([self.sums[index, spot][:2] for spot in spots])
        self.matrices = run_finish(blocks, self.layout, after)
        return self.matrices[0]


class Smalls:
    def __init__(self, landed, towers, axes):
        self.landed = landed
        self.towers = towers
        self.axes = list(axes) + [bit for bit in range(dp_bits()) if bit not in axes]
        self.values = None
        self.come = None
        self.hop = 0

    def step(self, index, stream, after):
        if self.values is None:
            members = [tower.small for tower in self.towers]
            rows = sum(member.shape[0] for member in members)
            self.values = run_rows(gather_kernel, members, rows, after)
        else:
            rows = self.values.shape[0]
            self.values = run_rows(add_kernel, [self.values, self.come], rows, after)
        axis = self.axes[self.hop]
        self.come = swap_cores(self.values) if axis is None else swap(self.values, axis)
        self.landed["s" + str(self.hop)] = self.come
        self.hop += 1
        return self.values

    def finish(self, index, stream, after):
        while self.hop < len(self.axes):
            self.step(0, 0, ())
        widths = [tower.layout.width for tower in self.towers]
        self.outs = run_small(
            self.values, self.come, widths, self.towers[0].depth_count, after
        )
        return self.outs[0]


STREAMS = {'i': ((0, 1), (2,), (3,)), 'c': ((0, 1, 2, 3),)}
WAYS = {
    "i": (
        ((1, 0, 2, 3), (2, 1, 0, 3), (2, 1, 0, 3)),
        ((1, 0, 2, 3), (0, 1, 2, 3), (2, 0, 1, 3)),
    ),
    "c": (
        ((1, 0, 2, 3),),
        ((2, 0, 1, 3),),
    ),
}
PLAN = (
    "kc00",
    "ki00",
    "fc00",
    "ss00",
    "fc10",
    "nc00",
    "ss00",
    "fi10+tc10",
    "ss00",
    "nc10",
    "ni10",
    "jc00",
    "fi00",
    "ss00",
    "jc10",
    "jc00",
    "ji11",
    "ni00",
    "jc10",
    "ji10",
    "ji11",
    "ji12",
    "ji02",
    "zc00",
    "ss00",
    "ji10",
    "ji00",
    "ji02",
    "zs00",
    "ji01",
    "ji12+gi103",
    "ji00",
    "ji01",
    "zi00",
)
SMALL_WAY = (0, None, 3, 2, 1)


def on_device(
    image_in,
    image_norm_gain,
    image_norm_shift,
    image_qkv,
    image_qv_bias,
    image_out_proj,
    image_fc_in,
    image_fc_in_bias,
    image_fc_out,
    image_res_bias,
    image_cot,
    caption_in,
    caption_norm_gain,
    caption_norm_shift,
    caption_qkv,
    caption_qv_bias,
    caption_out_proj,
    caption_fc_in,
    caption_fc_in_bias,
    caption_fc_out,
    caption_res_bias,
    caption_lengths,
    caption_cot,
):
    landed = {}
    depth_count = image_fc_in_bias.shape[0]
    members = (image_qv_bias, image_fc_in_bias, caption_qv_bias, caption_fc_in_bias)
    biases = jnp.concatenate([member.reshape(depth_count, -1) for member in members], axis=1)
    biases_far = swap_cores(biases)
    caption_bias_at = image_qv_bias[0].size + image_fc_in_bias[0].size
    image_own = (image_qkv, biases, image_out_proj, image_fc_in, image_fc_out)
    caption_own = (caption_qkv, biases, caption_out_proj, caption_fc_in, caption_fc_out)
    image_far = swap_all(image_own, "i", biases_far, landed)
    caption_far = swap_all(caption_own, "c", biases_far, landed)
    image_params = (
        image_norm_gain,
        image_norm_shift,
        image_res_bias,
        image_own,
        image_far,
        0,
    )
    caption_params = (
        caption_norm_gain,
        caption_norm_shift,
        caption_res_bias,
        caption_own,
        caption_far,
        caption_bias_at,
    )
    length = lax.dynamic_slice_in_dim(caption_lengths, lax.axis_index("tensor"), 1)
    caption = Tower(
        "c", landed, caption_in, caption_params, caption_cot, length, STREAMS["c"], WAYS["c"]
    )
    image = Tower("i", landed, image_in, image_params, image_cot, None, STREAMS["i"], WAYS["i"])
    smalls = Smalls(landed, (image, caption), SMALL_WAY)
    kinds = {
        "k": "whole",
        "f": "far_product",
        "n": "near_product",
        "j": "collect",
        "s": "step",
        "z": "finish",
    }
    towers = {"i": image, "c": caption, "s": smalls}
    after = caption_norm_gain
    for step in PLAN:
        name, *waits = step.split("+")
        member = towers[name[1]]
        before = [after] + [landed[wait] for wait in waits]
        after = getattr(member, kinds[name[0]])(int(name[2]), int(name[3]), before)
    outs = []
    for tower, few in ((image, smalls.outs[:5]), (caption, smalls.outs[5:])):
        matrix = tower.matrices
        outs += [
            tower.output,
            tower.grad,
            few[0],
            few[1],
            matrix[0],
            few[2],
            matrix[1],
            matrix[2],
            few[3],
            matrix[3],
            few[4],
        ]
    return tuple(outs)


def solution(mesh):
    placed = (
        P(("dp", "tensor"), None),
        P(),
        P(),
        P(None, None, None, "tensor"),
        P(None, None, "tensor"),
        P(None, "tensor", None),
        P(None, None, "tensor"),
        P(None, "tensor"),
        P(None, "tensor", None),
        P(),
        P(("dp", "tensor"), None),
        P(("dp", "tensor"), None),
        P(),
        P(),
        P(None, None, None, "tensor"),
        P(None, None, "tensor"),
        P(None, "tensor", None),
        P(None, None, "tensor"),
        P(None, "tensor"),
        P(None, "tensor", None),
        P(),
        P("dp"),
        P(("dp", "tensor"), None),
    )
    return jax.shard_map(
        on_device,
        mesh=mesh,
        in_specs=placed,
        out_specs=(
            P(("dp", "tensor"), None),
            P(("dp", "tensor"), None),
            P(),
            P(),
            P(None, None, "dp", "tensor"),
            P(),
            P(None, "tensor", "dp"),
            P(None, "dp", "tensor"),
            P(),
            P(None, "tensor", "dp"),
            P(),
            P(("dp", "tensor"), None),
            P(("dp", "tensor"), None),
            P(),
            P(),
            P(None, None, "dp", "tensor"),
            P(),
            P(None, "tensor", "dp"),
            P(None, "dp", "tensor"),
            P(),
            P(None, "tensor", "dp"),
            P(),
        ),
        check_vma=False,
    )
```
